32 devices in a mesh: brick: 8 (over y, x, core), scan: 4 (over z).
Axes of the slice: x: 2, y: 2, z: 4, core: 2. Of those that a mesh axis runs over, the one named last changes fastest.
Arguments:
- tomogram: bfloat16 [256, 128, 128], P(('brick', 'scan')), may hold values from -6 to 6
- deformed: bfloat16 [4, 256, 128, 128], P('scan', 'brick'), may hold values from -6 to 6
- subvoxel: float32 [4, 3, 8, 25], P('scan', None, 'brick'), may hold values from 0 to 0.99
- offsets: int32 [4, 3, 128], P('scan', None, 'brick'), may hold values from -15 to 15, as said below
Outputs:
- residual_map: bfloat16 [4, 256, 128, 128], P('scan', 'brick')
- node_rhs: float32 [4, 3, 8, 25], P('scan', None, 'brick')
The draws below stay inside these ranges and needn't reach their ends.
Inputs may be any that keep to these rules, and one draw needn't show every extreme that they name: offsets[k, c, e] lies in -(15) .. 15 and both ends occur.
All inputs are finite; a program needn't handle non-finite values.
Results may differ from the reference program's by a relative error of at most 0.0095.
Values may be sent and summed in bfloat16 or wider, within the bound.
No kernel may reach another device: no remote copies, remote signals or barrier semaphores. Data moves between devices by JAX's collectives and lax.ppermute only.
A program may use at most 128 MiB of HBM per device.

```python
import jax
import jax.numpy as jnp
from jax import lax

E = 32
HALO = 16
RADIUS = 3
NXY = 128
SCANS = 4
NZ = 256
EXY = 4
NODE_Z = 8
NODES_XY = 25
ELEMS = 128


def draw_offsets(key, part):
    base = jax.random.randint(key, (SCANS, 3, ELEMS), -(HALO - 1), HALO)
    spots = jax.random.randint(jax.random.fold_in(key, 7), (2,), 0, ELEMS)
    base = base.at[0, 0, spots[0]].set(HALO - 1)
    base = base.at[SCANS - 1, 0, spots[1]].set(-(HALO - 1))
    return base.astype(jnp.int32)


def level_of(stream_key, dims, cuts, smallest, high):
    gain = 1.0
    for dim, shards_of in cuts:
        draws = jax.random.uniform(jax.random.fold_in(jax.random.fold_in(stream_key, 6), dim), (shards_of,), jnp.float32, smallest / len(cuts), high / len(cuts))
        gain = gain * jnp.repeat(jnp.exp(draws), dims[dim] // shards_of).reshape((-1,) + (1,) * (len(dims) - 1 - dim))
    return gain


def centred(own_key, dims, scale, limit, cuts=(), kind=jnp.bfloat16):
    factor_of = level_of(own_key, dims, cuts, -0.22, 0.18) if cuts else 1.0
    values = jax.random.normal(own_key, dims, jnp.float32) * scale * factor_of
    return jnp.minimum(jnp.maximum(values, -limit), limit).astype(kind)


def setup_inputs(seed: int = 0) -> dict:
    key_of = jax.random.split(jax.random.key(seed), 5)
    tomogram = centred(key_of[0], (NZ, NXY, NXY), 1.0, 6.0, ((0, 32),))
    deformed = centred(key_of[1], (SCANS, NZ, NXY, NXY), 1.0, 6.0, ((0, 4), (1, 8)))
    subvoxel = jnp.clip(0.99 * jax.random.uniform(key_of[2], (SCANS, 3, NODE_Z, NODES_XY), jnp.float32) ** level_of(key_of[2], (SCANS, 3, NODE_Z, NODES_XY), ((0, 4), (2, 8)), -0.2, 0.2), 0.0, 0.99)
    offsets = draw_offsets(jax.random.fold_in(key_of[4], 71), 0)
    return {"tomogram": tomogram, "deformed": deformed, "subvoxel": subvoxel, "offsets": offsets}


gauss_sigma = 1.0


def filter_taps():
    tap_pos = jnp.arange(-RADIUS, RADIUS + 1).astype(jnp.float32)
    gaussian = jnp.exp(-tap_pos * tap_pos / (2.0 * gauss_sigma * gauss_sigma))
    smooth_taps = gaussian / jnp.sum(gaussian)
    slope_taps = tap_pos * gaussian / jnp.sum(tap_pos * tap_pos * gaussian)
    return smooth_taps.astype(jnp.bfloat16), slope_taps.astype(jnp.bfloat16)


def band_matrix(coeff, cross_width):
    distance = jnp.arange(cross_width)[:, None] - jnp.arange(cross_width)[None, :]
    band_table = jnp.zeros((cross_width, cross_width), jnp.float32)
    for tap in range(2 * RADIUS + 1):
        band_table = band_table + jnp.where(distance == tap - RADIUS, coeff[tap].astype(jnp.float32), jnp.float32(0.0))
    return band_table.astype(jnp.bfloat16)


def z_stencil(field, coeff, planes):
    stencil_sum = jnp.zeros((planes,) + field.shape[1:], jnp.float32)
    for tap in range(2 * RADIUS + 1):
        stencil_sum = stencil_sum + coeff[tap].astype(jnp.float32) * field[tap:tap + planes].astype(jnp.float32)
    return stencil_sum.astype(jnp.bfloat16)


def gradients(extended):
    smooth_taps, slope_taps = filter_taps()
    cross_width = extended.shape[2]
    planes = extended.shape[0] - 2 * RADIUS
    along_s = band_matrix(smooth_taps, cross_width)
    along_d = band_matrix(slope_taps, cross_width)
    both_bands = jnp.concatenate([along_s, along_d], axis=1)
    x_filtered = jnp.dot(extended.reshape(-1, cross_width), both_bands, preferred_element_type=jnp.float32)
    x_filtered = x_filtered.astype(jnp.bfloat16).reshape(extended.shape[0], extended.shape[1], 2 * cross_width)
    y_smoothed = jnp.einsum('zyx,yw->zwx', x_filtered.astype(jnp.float32), along_s.astype(jnp.float32)).astype(jnp.bfloat16)
    y_slope = jnp.einsum('zyx,yw->zwx', x_filtered[:, :, :cross_width].astype(jnp.float32), along_d.astype(jnp.float32)).astype(jnp.bfloat16)
    grad_z = z_stencil(y_smoothed[:, :, :cross_width], slope_taps, planes)
    grad_y = z_stencil(y_slope, smooth_taps, planes)
    grad_x = z_stencil(y_smoothed[:, :, cross_width:], smooth_taps, planes)
    return grad_z, grad_y, grad_x


def shape_table(edge_len):
    position = (jnp.arange(edge_len).astype(jnp.float32) + 0.5) / edge_len
    return jnp.stack([1.0 - position, position], axis=1)


def layer_terms(padded, z_start, ref_layer, grad_layer, node_pair, layer_offsets):
    edge_len = ref_layer.shape[0]
    cross_width = ref_layer.shape[1]
    per_row = cross_width // edge_len
    ref_blocks = ref_layer.reshape(edge_len, per_row, edge_len, per_row, edge_len).transpose(1, 3, 0, 2, 4)
    ref_blocks = ref_blocks.reshape(per_row * per_row, edge_len, edge_len, edge_len)
    grad_blocks = grad_layer.reshape(3, edge_len, per_row, edge_len, per_row, edge_len).transpose(2, 4, 0, 1, 3, 5)
    grad_blocks = grad_blocks.reshape(per_row * per_row, 3, edge_len, edge_len, edge_len)
    picked_nodes = []
    for j in range(2):
        for k in range(2):
            picked_nodes.append(node_pair[:, :, j:j + per_row, k:k + per_row])
    corner_nodes = jnp.stack(picked_nodes, axis=2).reshape(3, 2, 2, 2, per_row, per_row)
    corner_nodes = corner_nodes.transpose(4, 5, 0, 1, 2, 3).reshape(per_row * per_row, 3, 2, 2, 2)
    element_ids = jnp.arange(per_row * per_row, dtype=jnp.int32)
    starts_z = z_start + layer_offsets[0] + HALO
    starts_y = (element_ids // per_row) * edge_len + layer_offsets[1] + HALO
    starts_x = (element_ids % per_row) * edge_len + layer_offsets[2] + HALO

    def cut_window(start_z, start_y, start_x):
        return lax.dynamic_slice(padded, (start_z, start_y, start_x), (edge_len + 1, edge_len + 1, edge_len + 1))

    windows = jax.vmap(cut_window)(starts_z, starts_y, starts_x).astype(jnp.float32)
    shapes = shape_table(edge_len)
    subvoxel_field = jnp.einsum('enijk,ai,bj,ck->enabc', corner_nodes, shapes, shapes, shapes, precision=lax.Precision.HIGHEST)
    warped = jnp.zeros((per_row * per_row, edge_len, edge_len, edge_len), jnp.float32)
    for corner_z in range(2):
        weight_z = subvoxel_field[:, 0] if corner_z else 1.0 - subvoxel_field[:, 0]
        for corner_y in range(2):
            weight_y = subvoxel_field[:, 1] if corner_y else 1.0 - subvoxel_field[:, 1]
            for corner_x in range(2):
                weight_x = subvoxel_field[:, 2] if corner_x else 1.0 - subvoxel_field[:, 2]
                sample = windows[:, corner_z:corner_z + edge_len, corner_y:corner_y + edge_len, corner_x:corner_x + edge_len]
                warped = warped + weight_z * weight_y * weight_x * sample
    misfit = warped - ref_blocks.astype(jnp.float32)
    products = grad_blocks.astype(jnp.float32) * misfit[:, None]
    element_rhs = jnp.einsum('enabc,ai,bj,ck->enijk', products, shapes, shapes, shapes, precision=lax.Precision.HIGHEST) * (1.0 / edge_len)
    misfit_layer = misfit.reshape(per_row, per_row, edge_len, edge_len, edge_len).transpose(2, 0, 3, 1, 4)
    misfit_layer = misfit_layer.reshape(edge_len, cross_width, cross_width)
    corner_sums = element_rhs.reshape(per_row, per_row, 3, 2, 2, 2)
    planes = jnp.zeros((3, 2, per_row + 1, per_row + 1), jnp.float32)
    for j in range(2):
        for k in range(2):
            placed = corner_sums[:, :, :, :, j, k].transpose(2, 3, 0, 1)
            planes = planes + jnp.pad(placed, ((0, 0), (0, 0), (j, 1 - j), (k, 1 - k)))
    return misfit_layer, planes.reshape(3, 2, (per_row + 1) * (per_row + 1))


def reference(tomogram, deformed, subvoxel, offsets):
    extended = jnp.pad(tomogram, ((RADIUS, RADIUS), (0, 0), (0, 0)))
    grad_z, grad_y, grad_x = gradients(extended)
    gradient_all = jnp.stack([grad_z, grad_y, grad_x])
    nodes_all = jnp.concatenate([subvoxel, jnp.zeros((SCANS, 3, 1, NODES_XY), jnp.float32)], axis=2)

    def one_scan(scan_items):
        volume, node_values, scan_offsets = scan_items
        padded = jnp.pad(volume, HALO)
        node_grid = node_values.reshape(3, NODE_Z + 1, EXY + 1, EXY + 1)

        def one_layer(layer_index):
            ref_layer = lax.dynamic_slice_in_dim(tomogram, layer_index * E, E, 0)
            grad_layer = lax.dynamic_slice_in_dim(gradient_all, layer_index * E, E, 1)
            node_pair = lax.dynamic_slice_in_dim(node_grid, layer_index, 2, 1)
            layer_offsets = lax.dynamic_slice_in_dim(scan_offsets, layer_index * EXY * EXY, EXY * EXY, 1)
            return layer_terms(padded, layer_index * E, ref_layer, grad_layer, node_pair, layer_offsets)

        misfits, planes = lax.map(one_layer, jnp.arange(NODE_Z, dtype=jnp.int32))
        residual_scan = misfits.reshape(NZ, NXY, NXY).astype(jnp.bfloat16)
        bottoms = planes[:, :, 0]
        tops = planes[:, :, 1]
        assembled = bottoms + jnp.concatenate([jnp.zeros_like(tops[:1]), tops[:-1]], axis=0)
        return residual_scan, assembled.transpose(1, 0, 2)

    residual_map, node_rhs = lax.map(one_scan, (deformed, nodes_all, offsets))
    return residual_map, node_rhs
```

```python
import functools

import jax
import jax.numpy as jnp
import numpy as np
from jax import lax
from jax.experimental import pallas as pl
from jax.experimental.pallas import tpu as pltpu
from jax.sharding import PartitionSpec as P

E = 32
HALO = 16
RADIUS = 3
N = 128
ROW = N // E
WIN = 48
ROWS = HALO + N + E


def taps():
    t = np.arange(-RADIUS, RADIUS + 1).astype(np.float32)
    g = np.exp(-t * t / np.float32(2.0))
    smooth = g / np.sum(g)
    slope = t * g / np.sum(t * t * g)
    return [np.asarray(v, jnp.bfloat16).astype(np.float32) for v in (smooth, slope)]


def band(coeff):
    out = np.zeros((N, N), np.float32)
    for tap in range(2 * RADIUS + 1):
        out += coeff[tap] * np.eye(N, k=RADIUS - tap, dtype=np.float32)
    return out


SMOOTH, SLOPE = taps()
BAND_S, BAND_D = band(SMOOTH), band(SLOPE)
X_BANDS = np.concatenate([BAND_S, BAND_D], axis=1)
Y_BANDS = np.concatenate([BAND_S.T, BAND_D.T], axis=0)


def hat_rows():
    out = np.zeros((8, N), np.float32)
    for v in range(N):
        p = np.float32((v % E + 0.5) / E)
        out[v // E, v] = 1 - p
        out[v // E + 1, v] = p
    return out


HATS = hat_rows()


def lane_position(shape, dim):
    v = lax.broadcasted_iota(jnp.int32, shape, dim)
    return ((v % E).astype(jnp.float32) + 0.5) * (1.0 / E)


def warp_kernel(offs, nodes, own, low, high, hats, warped, vol, lhs, s_val, s_dif, w_base, w_step):
    zero_top = jnp.zeros((HALO, N), jnp.float32)
    zero_end = jnp.zeros((E, N), jnp.float32)

    def fill(src, first, count):
        def step(i, c):
            vol[first + i, 0:HALO] = zero_top
            vol[first + i, HALO : HALO + N] = src[i].astype(jnp.float32)
            vol[first + i, HALO + N : ROWS] = zero_end
            return c

        lax.fori_loop(0, count, step, 0, unroll=2)

    fill(low, 0, HALO)
    fill(own, HALO, E)
    fill(high, HALO + E, HALO)

    py = lane_position((E, N), 0)
    for c in range(3):
        line = []
        for iz in range(2):
            rows = []
            for iy in range(ROW + 1):
                acc = None
                for ix in range(ROW + 1):
                    term = nodes[c, iz * 25 + iy * (ROW + 1) + ix] * hats[ix : ix + 1, :]
                    acc = term if acc is None else acc + term
                rows.append(acc)
            line.append(rows)
        for ey in range(ROW):
            lo = line[0][ey] + py * (line[0][ey + 1] - line[0][ey])
            up = line[1][ey] + py * (line[1][ey + 1] - line[1][ey])
            w_base[c, ey * E : (ey + 1) * E] = lo
            w_step[c, ey * E : (ey + 1) * E] = up - lo

    src_lane = lax.broadcasted_iota(jnp.int32, (N, N), 0)
    out_lane = lax.broadcasted_iota(jnp.int32, (N, N), 1)
    shift = src_lane - out_lane
    block = out_lane // E

    def element_row(ey, carry):
        mats = []
        for ex in range(ROW):
            e = ey * ROW + ex
            oz, oy, ox = offs[0, e], offs[1, e], offs[2, e]
            mine = block == ex
            here = jnp.where(mine & (shift == ox), 1.0, 0.0)
            after = jnp.where(mine & (shift == ox + 1), 1.0, 0.0)
            mats.append(jnp.concatenate([here, after - here], axis=1).astype(jnp.bfloat16))
            first_z = oz + HALO
            first_y = ey * E + oy + HALO

            def copy_plane(z, c, ex=ex, first_z=first_z, first_y=first_y):
                lhs[z, :, ex * N : (ex + 1) * N] = vol[
                    first_z + z, pl.ds(first_y, WIN), :
                ].astype(jnp.bfloat16)
                return c

            lax.fori_loop(0, E + 1, copy_plane, 0, unroll=3)
        select = jnp.concatenate(mats, axis=0)

        def product(i, c):
            out = jnp.dot(
                lhs[pl.ds(i * 11, 11)].reshape(11 * WIN, ROW * N),
                select,
                preferred_element_type=jnp.float32,
            )
            s_val[pl.ds(i * 11, 11)] = out[:, :N].reshape(11, WIN, N)
            s_dif[pl.ds(i * 11, 11)] = out[:, N:].reshape(11, WIN, N)
            return c

        lax.fori_loop(0, 3, product, 0)

        def rows_of(r, c):
            base = pl.multiple_of(r * 8, 8)
            at = pl.multiple_of(ey * E + r * 8, 8)
            wz0, wy0, wx0 = [w_base[k, pl.ds(at, 8)] for k in range(3)]
            wz1, wy1, wx1 = [w_step[k, pl.ds(at, 8)] for k in range(3)]

            def corners(z):
                return (
                    s_val[z, pl.ds(base, 8)],
                    s_dif[z, pl.ds(base, 8)],
                    s_val[z, pl.ds(base + 1, 8)],
                    s_dif[z, pl.ds(base + 1, 8)],
                )

            below = corners(0)
            for z in range(E):
                above = corners(z + 1)
                p = (z + 0.5) / E
                wz = wz0 + p * wz1
                wy = wy0 + p * wy1
                wx = wx0 + p * wx1
                lines = []
                for v0, d0, v1, d1 in (below, above):
                    a0 = v0 + wx * d0
                    a1 = v1 + wx * d1
                    lines.append(a0 + wy * (a1 - a0))
                warped[z, pl.ds(at, 8)] = lines[0] + wz * (lines[1] - lines[0])
                below = above
            return c

        lax.fori_loop(0, E // 8, rows_of, 0)
        return carry

    lax.fori_loop(0, ROW, element_row, 0)


def warp(offs, nodes, own, low, high):
    vmem = pl.BlockSpec(memory_space=pltpu.VMEM)
    smem = pl.BlockSpec(memory_space=pltpu.SMEM)
    return pl.pallas_call(
        warp_kernel,
        out_shape=jax.ShapeDtypeStruct((E, N, N), jnp.float32),
        in_specs=[smem, smem, vmem, vmem, vmem, vmem],
        out_specs=vmem,
        scratch_shapes=[
            pltpu.VMEM((E + 2 * HALO, ROWS, N), jnp.float32),
            pltpu.VMEM((E + 1, WIN, ROW * N), jnp.bfloat16),
            pltpu.VMEM((E + 1, WIN, N), jnp.float32),
            pltpu.VMEM((E + 1, WIN, N), jnp.float32),
            pltpu.VMEM((3, N, N), jnp.float32),
            pltpu.VMEM((3, N, N), jnp.float32),
        ],
        compiler_params=pltpu.CompilerParams(vmem_limit_bytes=48 * 1024 * 1024),
        name="warp",
    )(offs, nodes, own, low, high, jnp.asarray(HATS))


def rhs_kernel(
    place, b0, b1, b2, b3, low, high, warped, x_bands, y_bands, hats,
    residual, bottom, top,
    y_z, y_y, y_x, misfit, sums,
):
    me = place[0]
    bands = x_bands[...]
    rows_s = y_bands[0:N]
    rows_d = y_bands[N : 2 * N]

    def filtered(src, count, at):
        flat = src[...].reshape(count * N, N)
        xf = jnp.dot(flat, bands, preferred_element_type=jnp.float32).astype(jnp.bfloat16)
        for i in range(count):
            plane = xf[i * N : (i + 1) * N]
            both = jnp.dot(rows_s, plane, preferred_element_type=jnp.float32)
            y_z[at + i] = both[:, :N]
            y_x[at + i] = both[:, N:]
            y_y[at + i] = jnp.dot(rows_d, plane[:, :N], preferred_element_type=jnp.float32)

    blocks = (b0, b1, b2, b3)
    depth = b0.shape[0]
    for j in range(4):
        first = (me ^ j) * depth
        filtered(blocks[j], depth, first + RADIUS)

        def differences(i, c, j=j, first=first):
            m = warped[first + i] - blocks[j][i].astype(jnp.float32)
            misfit[first + i] = m
            residual[first + i] = m.astype(jnp.bfloat16)
            return c

        lax.fori_loop(0, depth, differences, 0)
    filtered(low, RADIUS, 0)
    filtered(high, RADIUS, E + RADIUS)

    sums[...] = jnp.zeros_like(sums)
    smooth = [float(SMOOTH[RADIUS + t] / SMOOTH[RADIUS]) for t in range(RADIUS + 1)]
    slope = [float(SLOPE[RADIUS + t] / SLOPE[RADIUS + 1]) for t in range(RADIUS + 1)]

    def rows_of(r, carry):
        at = pl.multiple_of(r * 8, 8)
        ey = r // (E // 8)
        fields = (y_z, y_y, y_x)
        window = [[f[i, pl.ds(at, 8)] for i in range(2 * RADIUS)] for f in fields]
        zero = jnp.zeros((8, N), jnp.float32)
        plain = [zero] * 3
        running = [zero] * 3
        for z in range(E):
            for k in range(3):
                window[k] = window[k] + [fields[k][z + 2 * RADIUS, pl.ds(at, 8)]]
            m = misfit[z, pl.ds(at, 8)]
            w = window[0]
            grads = [
                (w[4] - w[2]) + slope[2] * (w[5] - w[1]) + slope[3] * (w[6] - w[0])
            ]
            for k in (1, 2):
                w = window[k]
                grads.append(
                    w[3]
                    + smooth[1] * (w[4] + w[2])
                    + smooth[2] * (w[5] + w[1])
                    + smooth[3] * (w[6] + w[0])
                )
            for k in range(3):
                plain[k] = plain[k] + grads[k] * m
                running[k] = running[k] + plain[k]
                window[k] = window[k][1:]
        row = lax.broadcasted_iota(jnp.int32, (8, N), 0) + (r % (E // 8)) * 8
        py = (row.astype(jnp.float32) + 0.5) * (1.0 / E)
        for k in range(3):
            gain = float(SLOPE[RADIUS + 1] if k == 0 else SMOOTH[RADIUS]) / E
            upper = (plain[k] * (1.0 + 0.5 / E) - running[k] * (1.0 / E)) * gain
            lower = plain[k] * gain - upper
            for iz, part in enumerate((lower, upper)):
                right = jnp.sum(part * py, axis=0, keepdims=True)
                left = jnp.sum(part, axis=0, keepdims=True) - right
                q = iz * 3 + k
                sums[q, pl.ds(ey, 1)] += left
                sums[q, pl.ds(ey + 1, 1)] += right
        return carry

    lax.fori_loop(0, N // 8, rows_of, 0)
    out = lax.dot_general(
        sums[...].reshape(48, N),
        hats[...],
        (((1,), (1,)), ((), ())),
        precision=lax.Precision.HIGHEST,
        preferred_element_type=jnp.float32,
    ).reshape(6, 8, 8)
    bottom[...] = out[:3]
    top[...] = out[3:]


def assemble(place, blocks, low, high, warped):
    vmem = pl.BlockSpec(memory_space=pltpu.VMEM)
    smem = pl.BlockSpec(memory_space=pltpu.SMEM)
    small = jax.ShapeDtypeStruct((3, 8, 8), jnp.float32)
    return pl.pallas_call(
        rhs_kernel,
        out_shape=(jax.ShapeDtypeStruct((E, N, N), jnp.bfloat16), small, small),
        in_specs=[smem] + [vmem] * 10,
        out_specs=(vmem, vmem, vmem),
        scratch_shapes=[pltpu.VMEM((E + 2 * RADIUS, N, N), jnp.float32)] * 3
        + [pltpu.VMEM((E, N, N), jnp.float32), pltpu.VMEM((6, 8, N), jnp.float32)],
        compiler_params=pltpu.CompilerParams(vmem_limit_bytes=48 * 1024 * 1024),
        name="rhs",
    )(
        place, *blocks, low, high, warped,
        jnp.asarray(X_BANDS, jnp.bfloat16), jnp.asarray(Y_BANDS, jnp.bfloat16), jnp.asarray(HATS),
    )


def chain(count, distance):
    return [(i, i + distance) for i in range(count) if 0 <= i + distance < count]


def body(tomogram, deformed, subvoxel, offsets):
    bricks = lax.axis_size("brick")
    me = lax.axis_index("scan")
    up, down = chain(bricks, 1), chain(bricks, -1)

    across = lax.ppermute(tomogram, "scan", [(0, 2), (1, 3), (2, 0), (3, 1)])
    beside = lax.ppermute(tomogram, "scan", [(0, 1), (1, 0), (2, 3), (3, 2)])
    slab = deformed[0]
    low = lax.ppermute(slab[E - HALO :], "brick", up)
    high = lax.ppermute(slab[:HALO], "brick", down)
    node_above = lax.ppermute(subvoxel, "brick", down)
    middle = lax.ppermute(tomogram, "scan", [(1, 2), (2, 1)])
    relayed = lax.ppermute(across, "scan", [(2, 3), (1, 0)])
    inner = (me == 1) | (me == 2)
    last = jnp.where(inner, middle, relayed)
    blocks = (tomogram, beside, across, last)

    nodes = jnp.concatenate([subvoxel[0, :, 0], node_above[0, :, 0]], axis=1)
    warped = warp(offsets[0], nodes, slab, low, high)

    def pick(index, part):
        out = part(blocks[0])
        for j in range(1, 4):
            out = jnp.where((me ^ j) == index, part(blocks[j]), out)
        return out

    low_ref = lax.ppermute(pick(3, lambda b: b[-RADIUS:]), "brick", up)
    high_ref = lax.ppermute(pick(0, lambda b: b[:RADIUS]), "brick", down)
    residual, bottom, top = assemble(me.reshape(1), blocks, low_ref, high_ref, warped)
    total = bottom + lax.ppermute(top, "brick", up)
    node_rhs = total[:, : ROW + 1, : ROW + 1].reshape(1, 3, 1, (ROW + 1) ** 2)
    return residual[None], node_rhs


def solution(mesh):
    return jax.shard_map(
        body,
        mesh=mesh,
        in_specs=(
            P(("brick", "scan"), None, None),
            P("scan", "brick", None, None),
            P("scan", None, "brick", None),
            P("scan", None, "brick"),
        ),
        out_specs=(P("scan", "brick", None, None), P("scan", None, "brick", None)),
        check_vma=False,
    )
```

```python
import functools

import jax
import jax.numpy as jnp
import numpy as np
from jax import lax
from jax.experimental import pallas as pl
from jax.experimental.pallas import tpu as pltpu
from jax.sharding import PartitionSpec as P

E = 32
HALO = 16
RADIUS = 3
N = 128
ROW = N // E
WIN = 48
HALF = E // 2
HALF_HALO = HALO // 2
ROWS = HALO + N + E


def taps():
    t = np.arange(-RADIUS, RADIUS + 1).astype(np.float32)
    g = np.exp(-t * t / np.float32(2.0))
    smooth = g / np.sum(g)
    slope = t * g / np.sum(t * t * g)
    return [np.asarray(v, jnp.bfloat16).astype(np.float32) for v in (smooth, slope)]


def band(coeff):
    out = np.zeros((N, N), np.float32)
    for tap in range(2 * RADIUS + 1):
        out += coeff[tap] * np.eye(N, k=RADIUS - tap, dtype=np.float32)
    return out


SMOOTH, SLOPE = taps()
BAND_S, BAND_D = band(SMOOTH), band(SLOPE)
X_BANDS = np.concatenate([BAND_S, BAND_D], axis=1)
Y_BANDS = np.concatenate([BAND_S.T, BAND_D.T], axis=0)


def rhs_hats():
    at = (np.arange(N, dtype=np.float32) + 0.5) / E
    hats = np.maximum(0.0, 1.0 - np.abs(at[:, None] - np.arange(ROW + 1, dtype=np.float32)))
    out = np.zeros((ROW + 1, N, N), np.float32)
    for iy in range(ROW + 1):
        out[iy, :, iy * (ROW + 1) : (iy + 1) * (ROW + 1)] = hats
    return out


RHS_HATS = rhs_hats()


def lane_position(shape, dim):
    v = lax.broadcasted_iota(jnp.int32, shape, dim)
    return ((v % E).astype(jnp.float32) + 0.5) * (1.0 / E)


def split_kernel(place, nodes_in, slab, near, far, far_end, nodes, wide, sems):
    odd = place[1]
    parts = ((1 - odd, 0, HALO, near), (odd, 0, HALF_HALO, far), (odd, HALF_HALO, HALF_HALO, far_end))
    copies = [
        pltpu.make_async_copy(
            slab.at[0, pl.ds(HALO * first + skip, count)], out.at[pl.ds(0, count)], sems.at[i]
        )
        for i, (first, skip, count, out) in enumerate(parts)
    ]
    fetch = pltpu.make_async_copy(nodes_in, nodes, sems.at[3])
    fetch.start()
    for c in copies:
        c.start()
    fetch.wait()
    wide[...] = jnp.zeros_like(wide)
    for c in range(3):
        wide[c : c + 1, 0 : (ROW + 1) ** 2] = nodes[0, c]
    rest = wide[...]
    rows = []
    for _ in range(3):
        rows.append(rest.astype(jnp.bfloat16).astype(jnp.float32))
        rest = rest - rows[-1]
    rows = jnp.concatenate(rows + [rest], axis=0).astype(jnp.bfloat16)
    for out, last in ((near, HALO), (far_end, HALF_HALO)):
        out[last, 0 : 4 * 8] = rows
        out[last, 4 * 8 : N] = jnp.zeros((N - 4 * 8, N), jnp.bfloat16)
    for c in copies:
        c.wait()


def shifted(below, offs, middle, other, halo, vol, lhs, store):
    zero_top = jnp.zeros((HALO, N), jnp.float32)
    zero_end = jnp.zeros((E, N), jnp.float32)

    def fill(srcs, first):
        count = HALO // len(srcs)
        for part, src in enumerate(srcs):

            def step(i, c, src=src, at=first + part * count):
                vol[at + i, 0:HALO] = zero_top
                vol[at + i, HALO : HALO + N] = src[i].astype(jnp.float32)
                vol[at + i, HALO + N : ROWS] = zero_end
                return c

            lax.fori_loop(0, count, step, 0, unroll=4)

    fill(halo, jnp.where(below, 0, E))
    fill(middle, HALO)
    fill(other, jnp.where(below, E, 0))

    lane = lax.broadcasted_iota(jnp.int32, (WIN, N), 1)
    src_lane = lax.broadcasted_iota(jnp.int32, (N, N), 0)
    out_lane = lax.broadcasted_iota(jnp.int32, (N, N), 1)
    distance = src_lane - out_lane
    block = out_lane // E

    def element_row(ey, carry):
        first_z, first_y, shift = [], [], []
        for ex in range(ROW):
            e = ey * ROW + ex
            first_z.append(offs[0, 0, e] + HALO)
            first_y.append(ey * E + offs[1, 0, e] + HALO)
            shift.append(offs[2, 0, e])
        mats = []
        for ex in range(2):
            moved = jnp.where(block == ex, distance - shift[ex], N)
            moved = jnp.where(block == ex + 2, distance - shift[ex + 2], moved)
            here = jnp.where(moved == 0, 1.0, 0.0)
            mats.append(jnp.concatenate([here, jnp.where(moved == 1, 1.0, 0.0) - here], axis=1))
        select = jnp.concatenate(mats, axis=0).astype(jnp.bfloat16)

        for z in range(HALF + 1):
            part = [vol[first_z[ex] + z, pl.ds(first_y[ex], WIN), :] for ex in range(ROW)]
            lhs[z, :, :N] = jnp.where(lane < E + HALO, part[0], part[2]).astype(jnp.bfloat16)
            lhs[z, :, N:] = jnp.where(lane < 2 * E + HALO, part[1], part[3]).astype(jnp.bfloat16)

        out = jnp.dot(
            lhs[...].reshape((HALF + 1) * WIN, 2 * N), select, preferred_element_type=jnp.float32
        )
        store(ey, out.reshape(HALF + 1, WIN, 2 * N))
        return carry

    lax.fori_loop(0, ROW, element_row, 0)


def window_kernel(
    place, offs, near, far, far_end, halo, val_out, dif_out, vol, lhs, s_val, s_dif, sems
):
    def copies(ey):
        return [
            pltpu.make_async_copy(src.at[ey], out.at[ey], sems.at[i, ey])
            for i, (src, out) in enumerate(((s_val, val_out), (s_dif, dif_out)))
        ]

    def store(ey, out):
        s_val[ey] = out[:, : E + 8, :N]
        s_dif[ey] = out[:, : E + 8, N:]
        for c in copies(ey):
            c.start()

    shifted(place[1] == 1, offs, (near,), (far, far_end), (halo,), vol, lhs, store)
    for ey in range(ROW):
        for c in copies(ey):
            c.wait()


def node_rows(plane, hats):
    row = lax.broadcasted_iota(jnp.int32, (16, N), 0)
    mine = lax.broadcasted_iota(jnp.int32, (16, N), 1) // (ROW + 1) == row % (ROW + 1)
    component = row // (ROW + 1)
    out = jnp.zeros((16, N), jnp.float32)
    values = plane[0 : 4 * 8].astype(jnp.float32)
    for piece in range(3):
        v = values[piece * 8 : piece * 8 + 8]
        line = jnp.where(component == 0, v[0:1], jnp.where(component == 1, v[1:2], v[2:3]))
        line = jnp.where(mine, line, 0.0).astype(jnp.bfloat16)
        out = out + jnp.dot(line, hats, preferred_element_type=jnp.float32)
    return out


def warp_kernel(
    place, offs, near, far, far_end, near_halo, far_halo, far_halo_end, val_in, dif_in,
    warped, vol, lhs, s_val, s_dif, w_base, w_step, val_a, dif_a, sems,
):
    odd = place[1] == 1
    earlier = [
        pltpu.make_async_copy(src, out, sems.at[i])
        for i, (src, out) in enumerate(((val_in, val_a), (dif_in, dif_a)))
    ]
    for c in earlier:
        c.start()

    def store(ey, out):
        s_val[ey] = out[:, : E + 8, :N]
        s_dif[ey] = out[:, : E + 8, N:]

    halo = (far_halo, far_halo_end)
    shifted(jnp.logical_not(odd), offs, (far, far_end), (near,), halo, vol, lhs, store)

    node = lax.broadcasted_iota(jnp.int32, (N, N), 0)
    at = (lax.broadcasted_iota(jnp.int32, (N, N), 1).astype(jnp.float32) + 0.5) * (1.0 / E)
    hat = jnp.maximum(0.0, 1.0 - jnp.abs(at - (node % (ROW + 1)).astype(jnp.float32)))
    hats = jnp.where(node < (ROW + 1) ** 2, hat, 0.0).astype(jnp.bfloat16)
    lower = node_rows(near[HALO], hats)
    upper = jnp.where(
        odd, node_rows(far_halo_end[HALF_HALO], hats), node_rows(near_halo[HALO], hats)
    )
    py = lane_position((E, N), 0)
    for c in range(3):
        for ey in range(ROW):
            q = c * (ROW + 1) + ey
            lo = lower[q : q + 1] + py * (lower[q + 1 : q + 2] - lower[q : q + 1])
            up = upper[q : q + 1] + py * (upper[q + 1 : q + 2] - upper[q : q + 1])
            w_step[c, ey * E : (ey + 1) * E] = up - lo
            w_base[c, ey * E : (ey + 1) * E] = lo

    def interpolate(val, dif, first_plane):
        start = first_plane.astype(jnp.float32) * (1.0 / E)

        def rows_of(r, carry):
            ey = r // (E // 8)
            base = (r % (E // 8)) * 8
            at = pl.multiple_of(r * 8, 8)
            wz1, wy1, wx1 = [w_step[k, pl.ds(at, 8)] for k in range(3)]
            wz0, wy0, wx0 = [
                w_base[k, pl.ds(at, 8)] + start * w for k, w in enumerate((wz1, wy1, wx1))
            ]

            def corners(z):
                return (
                    val[ey, z, pl.ds(base, 8)],
                    dif[ey, z, pl.ds(base, 8)],
                    val[ey, z, pl.ds(base + 1, 8)],
                    dif[ey, z, pl.ds(base + 1, 8)],
                )

            lower = corners(0)
            for z in range(HALF):
                upper = corners(z + 1)
                p = (z + 0.5) / E
                wz = wz0 + p * wz1
                wy = wy0 + p * wy1
                wx = wx0 + p * wx1
                lines = []
                for v0, d0, v1, d1 in (lower, upper):
                    a0 = v0 + wx * d0
                    a1 = v1 + wx * d1
                    lines.append(a0 + wy * (a1 - a0))
                warped[first_plane + z, pl.ds(at, 8)] = lines[0] + wz * (lines[1] - lines[0])
                lower = upper
            return carry

        lax.fori_loop(0, N // 8, rows_of, 0)

    interpolate(s_val, s_dif, jnp.where(odd, HALF, 0))
    for c in earlier:
        c.wait()
    interpolate(val_a, dif_a, jnp.where(odd, 0, HALF))


VMEM = pl.BlockSpec(memory_space=pltpu.VMEM)
SMEM = pl.BlockSpec(memory_space=pltpu.SMEM)
HBM = pl.BlockSpec(memory_space=pltpu.HBM)
VOLUME = jax.ShapeDtypeStruct((E, N, N), jnp.float32)
SAMPLES = (ROW, HALF + 1, E + 8, N)
RESIDUAL = jax.ShapeDtypeStruct((E, N, N), jnp.bfloat16)
FILTERED = jax.ShapeDtypeStruct((3, E, N, N), jnp.float32)
SMALL = jax.ShapeDtypeStruct((3, 1, (ROW + 1) ** 2), jnp.float32)


def call(kernel, name, outs, smem, vmem, scratch, mib, hbm=(), out_spec=VMEM):
    specs = [SMEM] * len(smem) + [VMEM] * len(vmem)
    return pl.pallas_call(
        kernel,
        out_shape=outs,
        in_specs=specs + [HBM] * len(hbm),
        out_specs=jax.tree.map(lambda _: out_spec, outs),
        scratch_shapes=scratch,
        compiler_params=pltpu.CompilerParams(vmem_limit_bytes=mib * 1024 * 1024),
        name=name,
    )(*smem, *vmem, *hbm)


def split(place, nodes, slab):
    return call(
        split_kernel,
        "split",
        tuple(jax.ShapeDtypeStruct((n, N, N), jnp.bfloat16) for n in (HALO + 1, HALF_HALO, HALF_HALO + 1)),
        [place],
        [],
        [
            pltpu.VMEM((1, 3, 1, (ROW + 1) ** 2), jnp.float32),
            pltpu.VMEM((8, N), jnp.float32),
            pltpu.SemaphoreType.DMA((4,)),
        ],
        4,
        hbm=[nodes, slab],
    )


WINDOW_SCRATCH = [
    pltpu.VMEM((E + HALO, ROWS, N), jnp.float32),
    pltpu.VMEM((HALF + 1, WIN, 2 * N), jnp.bfloat16),
    pltpu.VMEM(SAMPLES, jnp.float32),
    pltpu.VMEM(SAMPLES, jnp.float32),
]


def windows(place, offs, *planes):
    samples = pltpu.HBM(SAMPLES, jnp.float32)
    return call(
        window_kernel,
        "windows",
        (samples, samples),
        [place, offs],
        planes,
        WINDOW_SCRATCH + [pltpu.SemaphoreType.DMA((2, ROW))],
        12,
        out_spec=HBM,
    )


def warp(place, offs, planes, samples):
    return call(
        warp_kernel,
        "warp",
        VOLUME,
        [place, offs],
        planes,
        WINDOW_SCRATCH
        + [pltpu.VMEM((3, N, N), jnp.float32)] * 2
        + [pltpu.VMEM(SAMPLES, jnp.float32)] * 2
        + [pltpu.SemaphoreType.DMA((2,))],
        16,
        hbm=samples,
    )


def filter_into(y, planes, at, x_bands, y_bands):
    smoothed, slopes = [], []
    for i in range(0, len(planes), 2):
        pair = planes[i : i + 2]
        both = jnp.concatenate(pair, axis=1) if len(pair) == 2 else pair[0]
        along_y = jnp.dot(y_bands[...], both, preferred_element_type=jnp.float32)
        along_y = along_y.astype(jnp.bfloat16)
        for k in range(len(pair)):
            smoothed.append(along_y[:N, k * N : (k + 1) * N])
            slopes.append(along_y[N:, k * N : (k + 1) * N])
    rows = pl.ds(at, len(planes))
    out = jnp.dot(jnp.concatenate(smoothed), x_bands[...], preferred_element_type=jnp.float32)
    y[0, rows] = out[:, :N].reshape(-1, N, N)
    y[2, rows] = out[:, N:].reshape(-1, N, N)
    out = jnp.dot(jnp.concatenate(slopes), x_bands[:, :N], preferred_element_type=jnp.float32)
    y[1, rows] = out.reshape(-1, N, N)


def filter_kernel(
    place, warped, x_bands, y_bands, b0, b1, b2, b3, misfit, residual, y, held, sems
):
    me = place[0]
    depth = b0.shape[0]
    copies = [
        pltpu.make_async_copy(b, held.at[j], sems.at[j]) for j, b in enumerate((b0, b1, b2, b3))
    ]
    for c in copies:
        c.start()
    for j in range(4):
        copies[j].wait()
        filter_into(y, [held[j, i] for i in range(depth)], j * depth, x_bands, y_bands)
        first = (me ^ j) * depth
        for i in range(depth):
            m = warped[first + i] - held[j, i].astype(jnp.float32)
            misfit[first + i] = m
            residual[first + i] = m.astype(jnp.bfloat16)


def filtered(place, blocks, warped):
    return call(
        filter_kernel,
        "filters",
        (VOLUME, RESIDUAL, FILTERED),
        [place],
        [warped, jnp.asarray(X_BANDS, jnp.bfloat16), jnp.asarray(Y_BANDS, jnp.bfloat16)],
        [pltpu.VMEM((4, E // 4, N, N), jnp.bfloat16), pltpu.SemaphoreType.DMA((4,))],
        24,
        hbm=blocks,
    )


def rhs_kernel(
    place, edge_a, edge_b, misfit, y, x_bands, y_bands, hats, bottom, top, edges, sums
):
    me, odd = place[0], place[1]
    depth = E // 4
    planes = [edge[i] for edge in (edge_a, edge_b) for i in range(RADIUS)]
    filter_into(edges, planes, 0, x_bands, y_bands)

    sums[...] = jnp.zeros_like(sums)
    smooth = [float(SMOOTH[RADIUS + t] / SMOOTH[RADIUS]) for t in range(RADIUS + 1)]
    slope = [float(SLOPE[RADIUS + t] / SLOPE[RADIUS + 1]) for t in range(RADIUS + 1)]
    below = RADIUS * (1 - odd)
    above = RADIUS * odd
    starts = [(me ^ j) * depth for j in range(4)]

    def plane(k, z, rows):
        if z < 0:
            return edges[k, below + RADIUS + z, rows]
        if z >= E:
            return edges[k, above + z - E, rows]
        return y[k, starts[z // depth] + z % depth, rows]

    def rows_of(r, carry):
        at = pl.multiple_of(r * 8, 8)
        ey = r // (E // 8)
        rows = pl.ds(at, 8)
        window = [[plane(k, z, rows) for z in range(-RADIUS, RADIUS)] for k in range(3)]
        zero = jnp.zeros((8, N), jnp.float32)
        plain = [zero] * 3
        running = [zero] * 3
        for z in range(E):
            for k in range(3):
                window[k] = window[k] + [plane(k, z + RADIUS, rows)]
            m = misfit[z, rows]
            w = window[0]
            grads = [(w[4] - w[2]) + slope[2] * (w[5] - w[1]) + slope[3] * (w[6] - w[0])]
            for k in (1, 2):
                w = window[k]
                grads.append(
                    w[3]
                    + smooth[1] * (w[4] + w[2])
                    + smooth[2] * (w[5] + w[1])
                    + smooth[3] * (w[6] + w[0])
                )
            for k in range(3):
                plain[k] = plain[k] + grads[k] * m
                running[k] = running[k] + plain[k]
                window[k] = window[k][1:]
        row = lax.broadcasted_iota(jnp.int32, (8, N), 0) + (r % (E // 8)) * 8
        py = (row.astype(jnp.float32) + 0.5) * (1.0 / E)
        for k in range(3):
            gain = float(SLOPE[RADIUS + 1] if k == 0 else SMOOTH[RADIUS]) / E
            upper = (plain[k] * (1.0 + 0.5 / E) - running[k] * (1.0 / E)) * gain
            lower = plain[k] * gain - upper
            for iz, part in enumerate((lower, upper)):
                right = jnp.sum(part * py, axis=0, keepdims=True)
                left = jnp.sum(part, axis=0, keepdims=True) - right
                q = iz * 3 + k
                sums[ey, q : q + 1] += left
                sums[ey + 1, q : q + 1] += right
        return carry

    lax.fori_loop(0, N // 8, rows_of, 0)
    out = jnp.zeros((8, N), jnp.float32)
    for iy in range(ROW + 1):
        rest = sums[iy]
        for piece in range(3):
            part = rest.astype(jnp.bfloat16)
            rest = rest - part.astype(jnp.float32)
            out = out + jnp.dot(part, hats[iy], preferred_element_type=jnp.float32)
    for k in range(3):
        bottom[k] = out[k : k + 1, : (ROW + 1) ** 2]
        top[k] = out[3 + k : 4 + k, : (ROW + 1) ** 2]


def assemble(place, edges, misfit, y):
    return call(
        rhs_kernel,
        "rhs",
        (SMALL, SMALL),
        [place],
        [
            *edges, misfit, y,
            jnp.asarray(X_BANDS, jnp.bfloat16), jnp.asarray(Y_BANDS, jnp.bfloat16),
            jnp.asarray(RHS_HATS, jnp.bfloat16),
        ],
        [
            pltpu.VMEM((3, 2 * RADIUS, N, N), jnp.float32),
            pltpu.VMEM((ROW + 1, 8, N), jnp.float32),
        ],
        24,
    )


def body(tomogram, deformed, subvoxel, offsets):
    bricks = lax.axis_size("brick")
    me = lax.axis_index("scan")
    odd = lax.axis_index("brick") % 2
    place = jnp.stack([me, odd]).astype(jnp.int32)
    up = [(i, i + 1) for i in range(bricks - 1)]
    inside = [r for i in range(0, bricks - 1, 2) for r in ((i, i + 1), (i + 1, i))]
    outside = [r for i in range(1, bricks - 1, 2) for r in ((i, i + 1), (i + 1, i))]
    pairs = [(0, 1), (1, 0), (2, 3), (3, 2)]

    slab = pltpu.with_memory_space_constraint(deformed, pltpu.HBM)
    across = lax.ppermute(tomogram, "scan", [(0, 2), (1, 3), (2, 0), (3, 1)])
    near, far, far_end = split(place, pltpu.with_memory_space_constraint(subvoxel, pltpu.HBM), slab)
    offs = offsets.reshape(3, 1, -1)
    halo_a = lax.ppermute(near, "brick", inside)
    halo_b = lax.ppermute(far, "brick", outside)
    halo_c = lax.ppermute(far_end, "brick", outside)
    late = tomogram
    beside = lax.ppermute(late, "scan", pairs)
    samples = windows(place, offs, near, far, far_end, halo_a)
    across, samples = lax.optimization_barrier((across, samples))
    samples = [pltpu.with_memory_space_constraint(x, pltpu.HBM) for x in samples]
    relayed = lax.ppermute(across, "scan", pairs)
    blocks = (tomogram, beside, across, relayed)
    warped = warp(place, offs, (near, far, far_end, halo_a, halo_b, halo_c), samples)

    def pick(index, part):
        out = part(blocks[0])
        for j in range(1, 4):
            out = jnp.where((me ^ j) == index, part(blocks[j]), out)
        return out

    tail, head = pick(3, lambda b: b[-RADIUS:]), pick(0, lambda b: b[:RADIUS])
    send_a, send_b, warped = lax.optimization_barrier(
        (jnp.where(odd == 1, head, tail), jnp.where(odd == 1, tail, head), warped)
    )
    edges = (lax.ppermute(send_a, "brick", inside), lax.ppermute(send_b, "brick", outside))
    misfit, residual, y = filtered(place, blocks, warped)
    bottom, top = assemble(place, edges, misfit, y)
    node_rhs = bottom + lax.ppermute(top, "brick", up)
    return residual[None], node_rhs[None]


def solution(mesh):
    return jax.shard_map(
        body,
        mesh=mesh,
        in_specs=(
            P(("brick", "scan"), None, None),
            P("scan", "brick", None, None),
            P("scan", None, "brick", None),
            P("scan", None, "brick"),
        ),
        out_specs=(P("scan", "brick", None, None), P("scan", None, "brick", None)),
        check_vma=False,
    )
```

```python
import functools

import jax
import jax.numpy as jnp
import numpy as np
from jax import lax
from jax.experimental import pallas as pl
from jax.experimental.pallas import tpu as pltpu
from jax.sharding import PartitionSpec as P

E = 32
HALO = 16
RADIUS = 3
N = 128
ROW = N // E
WIN = 48
HALF = E // 2
FAR = HALO // 2
ROWS = HALO + N + E


def taps():
    t = np.arange(-RADIUS, RADIUS + 1).astype(np.float32)
    g = np.exp(-t * t / np.float32(2.0))
    smooth = g / np.sum(g)
    slope = t * g / np.sum(t * t * g)
    return [np.asarray(v, jnp.bfloat16).astype(np.float32) for v in (smooth, slope)]


def band(coeff):
    out = np.zeros((N, N), np.float32)
    for tap in range(2 * RADIUS + 1):
        out += coeff[tap] * np.eye(N, k=RADIUS - tap, dtype=np.float32)
    return out


SMOOTH, SLOPE = taps()
BAND_S, BAND_D = band(SMOOTH), band(SLOPE)
X_BANDS = np.concatenate(
    [
        np.concatenate([BAND_S, BAND_D], axis=1),
        np.concatenate([BAND_S, 0 * BAND_S], axis=1),
        np.concatenate([0 * BAND_S, BAND_S], axis=1),
    ]
)
Y_BANDS = np.concatenate([BAND_S.T, BAND_D.T], axis=0)


def rhs_hats():
    at = (np.arange(N, dtype=np.float32) + 0.5) / E
    hats = np.maximum(0.0, 1.0 - np.abs(at[:, None] - np.arange(ROW + 1, dtype=np.float32)))
    out = np.zeros((ROW + 1, N, N), np.float32)
    for iy in range(ROW + 1):
        out[iy, :, iy * (ROW + 1) : (iy + 1) * (ROW + 1)] = hats
    return out


RHS_HATS = rhs_hats()


def lane_position(shape, dim):
    v = lax.broadcasted_iota(jnp.int32, shape, dim)
    return ((v % E).astype(jnp.float32) + 0.5) * (1.0 / E)


def split_kernel(place, nodes_in, slab, near, far, far_end, nodes, wide, sems):
    odd = place[1]
    parts = ((1 - odd, 0, HALO, near), (odd, 0, FAR, far), (odd, FAR, HALO - FAR, far_end))
    copies = [
        pltpu.make_async_copy(
            slab.at[0, pl.ds(HALO * first + skip, count)], out.at[pl.ds(0, count)], sems.at[i]
        )
        for i, (first, skip, count, out) in enumerate(parts)
    ]
    fetch = pltpu.make_async_copy(nodes_in, nodes, sems.at[len(parts)])
    fetch.start()
    for c in copies:
        c.start()
    fetch.wait()
    wide[...] = jnp.zeros_like(wide)
    for c in range(3):
        wide[c : c + 1, 0 : (ROW + 1) ** 2] = nodes[0, c]
    rest = wide[...]
    rows = []
    for _ in range(3):
        rows.append(rest.astype(jnp.bfloat16).astype(jnp.float32))
        rest = rest - rows[-1]
    rows = jnp.concatenate(rows + [rest], axis=0).astype(jnp.bfloat16)
    for out, last in ((near, HALO), (far, FAR)):
        out[last, 0 : 4 * 8] = rows
        out[last, 4 * 8 : N] = jnp.zeros((N - 4 * 8, N), jnp.bfloat16)
    for c in copies:
        c.wait()


def shifted(below, offs, fetch, middle, other, halo, vol, lhs, s_val, s_dif, done=None):
    zero_top = jnp.zeros((HALO, N), jnp.float32)
    zero_end = jnp.zeros((E, N), jnp.float32)

    def fill(srcs, first):
        counts = (HALO,) if len(srcs) == 1 else (FAR, HALO - FAR)
        for src, count in zip(srcs, counts):

            def step(i, c, src=src, at=first):
                vol[at + i, 0:HALO] = zero_top
                vol[at + i, HALO : HALO + N] = src[i].astype(jnp.float32)
                vol[at + i, HALO + N : ROWS] = zero_end
                return c

            lax.fori_loop(0, count, step, 0, unroll=count // 2)
            first = first + count

    fill(halo, jnp.where(below, 0, E))
    fill(middle, HALO)
    fill(other, jnp.where(below, E, 0))
    fetch.wait()

    lane = lax.broadcasted_iota(jnp.int32, (WIN, N), 1)
    src_lane = lax.broadcasted_iota(jnp.int32, (N, N), 0)
    out_lane = lax.broadcasted_iota(jnp.int32, (N, N), 1)
    distance = src_lane - out_lane
    block = out_lane // E

    def element_row(ey):
        first_z, first_y, shift = [], [], []
        for ex in range(ROW):
            e = ey * ROW + ex
            first_z.append(offs[0, 0, e] + HALO)
            first_y.append(ey * E + offs[1, 0, e] + HALO)
            shift.append(offs[2, 0, e])
        mats = []
        for ex in range(2):
            moved = jnp.where(block == ex, distance - shift[ex], N)
            moved = jnp.where(block == ex + 2, distance - shift[ex + 2], moved)
            here = jnp.where(moved == 0, 1.0, 0.0)
            mats.append(jnp.concatenate([here, jnp.where(moved == 1, 1.0, 0.0) - here], axis=1))
        select = jnp.concatenate(mats, axis=0).astype(jnp.bfloat16)

        for z in range(HALF + 1):
            part = [vol[first_z[ex] + z, pl.ds(first_y[ex], WIN), :] for ex in range(ROW)]
            lhs[z, :, :N] = jnp.where(lane < E + HALO, part[0], part[2]).astype(jnp.bfloat16)
            lhs[z, :, N:] = jnp.where(lane < 2 * E + HALO, part[1], part[3]).astype(jnp.bfloat16)

        out = jnp.dot(
            lhs[...].reshape((HALF + 1) * WIN, 2 * N), select, preferred_element_type=jnp.float32
        )
        out = out.reshape(HALF + 1, WIN, 2 * N)
        s_val[ey] = out[:, : E + 8, :N]
        s_dif[ey] = out[:, : E + 8, N:]
        if done is not None:
            done(ey)

    for ey in range(ROW):
        element_row(ey)


def node_rows(plane, hats):
    row = lax.broadcasted_iota(jnp.int32, (16, N), 0)
    mine = lax.broadcasted_iota(jnp.int32, (16, N), 1) // (ROW + 1) == row % (ROW + 1)
    component = row // (ROW + 1)
    out = jnp.zeros((16, N), jnp.float32)
    values = plane[0 : 4 * 8].astype(jnp.float32)
    for piece in range(3):
        v = values[piece * 8 : piece * 8 + 8]
        line = jnp.where(component == 0, v[0:1], jnp.where(component == 1, v[1:2], v[2:3]))
        line = jnp.where(mine, line, 0.0).astype(jnp.bfloat16)
        out = out + jnp.dot(line, hats, preferred_element_type=jnp.float32)
    return out


def displacements(odd, near, near_halo, far_halo, w_base, w_step):
    node = lax.broadcasted_iota(jnp.int32, (N, N), 0)
    at = (lax.broadcasted_iota(jnp.int32, (N, N), 1).astype(jnp.float32) + 0.5) * (1.0 / E)
    hat = jnp.maximum(0.0, 1.0 - jnp.abs(at - (node % (ROW + 1)).astype(jnp.float32)))
    hats = jnp.where(node < (ROW + 1) ** 2, hat, 0.0).astype(jnp.bfloat16)
    lower = node_rows(near[HALO], hats)
    upper = node_rows(jnp.where(odd, far_halo[FAR], near_halo[HALO]), hats)
    py = lane_position((E, N), 0)
    for c in range(3):
        for ey in range(ROW):
            q = c * (ROW + 1) + ey
            lo = lower[q : q + 1] + py * (lower[q + 1 : q + 2] - lower[q : q + 1])
            up = upper[q : q + 1] + py * (upper[q + 1 : q + 2] - upper[q : q + 1])
            w_step[c, ey * E : (ey + 1) * E] = up - lo
            w_base[c, ey * E : (ey + 1) * E] = lo


def interpolate(val, dif, w_base, w_step, first_plane, warped, ey):
    start = first_plane.astype(jnp.float32) * (1.0 / E)

    for base in range(0, E, 8):
        at = ey * E + base
        wz1, wy1, wx1 = [w_step[k, pl.ds(at, 8)] for k in range(3)]
        wz0, wy0, wx0 = [
            w_base[k, pl.ds(at, 8)] + start * w for k, w in enumerate((wz1, wy1, wx1))
        ]

        def corners(z, base=base):
            return (
                val[ey, z, pl.ds(base, 8)],
                dif[ey, z, pl.ds(base, 8)],
                val[ey, z, pl.ds(base + 1, 8)],
                dif[ey, z, pl.ds(base + 1, 8)],
            )

        lower = corners(0)
        for z in range(HALF):
            upper = corners(z + 1)
            p = (z + 0.5) / E
            wz = wz0 + p * wz1
            wy = wy0 + p * wy1
            wx = wx0 + p * wx1
            lines = []
            for v0, d0, v1, d1 in (lower, upper):
                a0 = v0 + wx * d0
                a1 = v1 + wx * d1
                lines.append(a0 + wy * (a1 - a0))
            warped[z, pl.ds(at, 8)] = lines[0] + wz * (lines[1] - lines[0])
            lower = upper


def window_kernel(
    place, near, far, far_end, near_halo, offs_in,
    val_out, dif_out, vol, lhs, s_val, s_dif, offs, sem, sems,
):
    fetch = pltpu.make_async_copy(offs_in, offs, sem)
    fetch.start()

    def copies(ey):
        return [
            pltpu.make_async_copy(src.at[ey], out.at[ey], sems.at[i, ey])
            for i, (src, out) in enumerate(((s_val, val_out), (s_dif, dif_out)))
        ]

    def done(ey):
        for c in copies(ey):
            c.start()

    shifted(
        place[1] == 1, offs, fetch, (near,), (far, far_end), (near_halo,), vol, lhs, s_val, s_dif, done
    )
    for ey in range(ROW):
        for c in copies(ey):
            c.wait()


def first_kernel(
    place, near, near_halo, far_halo, val_in, dif_in, warped, w_base, w_step, val, dif, sems
):
    copies = [
        [
            pltpu.make_async_copy(src.at[ey], out.at[ey], sems.at[i, ey])
            for i, (src, out) in enumerate(((val_in, val), (dif_in, dif)))
        ]
        for ey in range(ROW)
    ]
    for pair in copies:
        for c in pair:
            c.start()
    odd = place[1] == 1
    displacements(odd, near, near_halo, far_halo, w_base, w_step)
    for ey, pair in enumerate(copies):
        for c in pair:
            c.wait()
        interpolate(val, dif, w_base, w_step, jnp.where(odd, 0, HALF), warped, ey)


def second_kernel(
    place, near, far, far_end, far_halo, far_halo_end, w_base, w_step,
    warp_a, b0, b1, x_bands, y_bands, offs_in,
    warped, residual, y, misfit, vol, lhs, s_val, s_dif, offs, sem, rounded, out_sem,
):
    odd = place[1] == 1
    fetch = pltpu.make_async_copy(offs_in, offs, sem)
    fetch.start()
    halo = (far_halo, far_halo_end)
    shifted(
        jnp.logical_not(odd), offs, fetch, (far, far_end), (near,), halo, vol, lhs, s_val, s_dif
    )
    for ey in range(ROW):
        interpolate(s_val, s_dif, w_base, w_step, jnp.where(odd, HALF, 0), warped, ey)
    filter_half(
        (0, 1), place, warp_a, warped, (b0, b1), x_bands, y_bands,
        residual, y, misfit, rounded, out_sem,
    ).wait()


VMEM = pl.BlockSpec(memory_space=pltpu.VMEM)
SMEM = pl.BlockSpec(memory_space=pltpu.SMEM)
HBM = pl.BlockSpec(memory_space=pltpu.HBM)
FIELD = jax.ShapeDtypeStruct((3, N, N), jnp.float32)
HALF_VOLUME = jax.ShapeDtypeStruct((HALF, N, N), jnp.float32)
SAMPLES = (ROW, HALF + 1, E + 8, N)
RESIDUAL = jax.ShapeDtypeStruct((E, N, N), jnp.bfloat16)
FILTERED = jax.ShapeDtypeStruct((3, HALF, N, N), jnp.float32)
SMALL = jax.ShapeDtypeStruct((3, 1, (ROW + 1) ** 2), jnp.float32)


def call(kernel, name, outs, smem, vmem, scratch, mib, hbm=(), hbm_outs=(), alias=None):
    specs = [SMEM] * len(smem) + [VMEM] * len(vmem)
    return pl.pallas_call(
        kernel,
        out_shape=outs,
        in_specs=specs + [HBM] * len(hbm),
        out_specs=tuple(HBM if i in hbm_outs else VMEM for i in range(len(outs))),
        input_output_aliases=alias or {},
        scratch_shapes=scratch,
        compiler_params=pltpu.CompilerParams(vmem_limit_bytes=mib * 1024 * 1024),
        name=name,
    )(*smem, *vmem, *hbm)


def split(place, nodes, slab):
    return call(
        split_kernel,
        "split",
        tuple(jax.ShapeDtypeStruct((n, N, N), jnp.bfloat16) for n in (HALO + 1, FAR + 1, HALO - FAR)),
        [place],
        [],
        [
            pltpu.VMEM((1, 3, 1, (ROW + 1) ** 2), jnp.float32),
            pltpu.VMEM((8, N), jnp.float32),
            pltpu.SemaphoreType.DMA((4,)),
        ],
        4,
        hbm=[nodes, slab],
    )


SAMPLE_SCRATCH = [pltpu.VMEM(SAMPLES, jnp.float32)] * 2
WINDOW_SCRATCH = [
    pltpu.VMEM((E + HALO, ROWS, N), jnp.float32),
    pltpu.VMEM((HALF + 1, WIN, 2 * N), jnp.bfloat16),
    *SAMPLE_SCRATCH,
    pltpu.SMEM((3, 1, ROW * ROW), jnp.int32),
    pltpu.SemaphoreType.DMA,
]
EACH_ROW = pltpu.SemaphoreType.DMA((2, ROW))


def windows(place, offs, planes):
    out = pltpu.HBM(SAMPLES, jnp.float32)
    scratch = WINDOW_SCRATCH + [EACH_ROW]
    return call(
        window_kernel, "windows", (out, out), [place], planes, scratch, 20, hbm=[offs], hbm_outs=(0, 1)
    )


def first_half(place, planes, samples):
    samples = [pltpu.with_memory_space_constraint(x, pltpu.HBM) for x in samples]
    scratch = SAMPLE_SCRATCH + [EACH_ROW]
    outs = (HALF_VOLUME, FIELD, FIELD)
    return call(first_kernel, "first_half", outs, [place], planes, scratch, 16, hbm=samples)


ROUNDED = [pltpu.VMEM((HALF, N, N), jnp.bfloat16), pltpu.SemaphoreType.DMA]


def bands():
    return jnp.asarray(X_BANDS, jnp.bfloat16), jnp.asarray(Y_BANDS, jnp.bfloat16)


def second_half(place, offs, planes, warp_a, blocks):
    return call(
        second_kernel,
        "second_half",
        (HALF_VOLUME, RESIDUAL, FILTERED, HALF_VOLUME),
        [place],
        [*planes, warp_a, *blocks, *bands()],
        WINDOW_SCRATCH + ROUNDED,
        32,
        hbm=[offs],
        hbm_outs=(1,),
    )


def filter_into(y, planes, at, x_bands, y_bands):
    count = len(planes)
    smoothed, slopes = [], []
    for i in range(0, count, 2):
        pair = jnp.concatenate(planes[i : i + 2], axis=1)
        along_y = jnp.dot(y_bands[...], pair, preferred_element_type=jnp.float32)
        along_y = along_y.astype(jnp.bfloat16)
        smoothed += [along_y[:N, :N], along_y[:N, N:]]
        slopes.append(along_y[N:])
    rows = pl.ds(at, count)
    out = jnp.dot(jnp.concatenate(smoothed), x_bands[0:N], preferred_element_type=jnp.float32)
    y[0, rows] = out[:, :N].reshape(-1, N, N)
    y[2, rows] = out[:, N:].reshape(-1, N, N)
    out = jnp.dot(jnp.concatenate(slopes), x_bands[N:], preferred_element_type=jnp.float32)
    for i in range(count):
        y[1, at + i] = out[i // 2 * N : i // 2 * N + N, i % 2 * N : i % 2 * N + N]


def filter_half(
    slots, place, warp_a, warp_b, blocks, x_bands, y_bands, residual, y, misfit, rounded, sem
):
    me, odd = place[0], place[1]
    depth = blocks[0].shape[0]
    half = (me ^ slots[0]) // 2

    def subtract(warped):
        for j, b in zip(slots, blocks):
            at = ((me ^ j) % 2) * depth
            for i in range(depth):
                m = warped[at + i] - b[i].astype(jnp.float32)
                misfit[at + i] = m
                rounded[at + i] = m.astype(jnp.bfloat16)

    pl.when(half + odd == 1)(lambda: subtract(warp_a))
    pl.when(half + odd != 1)(lambda: subtract(warp_b))
    out = pltpu.make_async_copy(rounded, residual.at[pl.ds(half * HALF, HALF)], sem)
    out.start()
    for j, b in zip(slots, blocks):
        at = ((me ^ j) % 2) * depth
        filter_into(y, [b[i] for i in range(depth)], at, x_bands, y_bands)
    return out


def add_up(sums, odd, y, misfit, edges, ranges):
    smooth = [float(SMOOTH[RADIUS + t] / SMOOTH[RADIUS]) for t in range(RADIUS + 1)]
    slope = [float(SLOPE[RADIUS + t] / SLOPE[RADIUS + 1]) for t in range(RADIUS + 1)]
    below = RADIUS * (1 - odd)
    above = RADIUS * odd

    def plane(k, z, rows):
        if z < 0:
            return edges[k, below + RADIUS + z, rows]
        if z >= E:
            return edges[k, above + z - E, rows]
        return y[z // HALF][k, z % HALF, rows]

    def planes_of(rows, begin, end):
        window = [[plane(k, begin + t, rows) for t in range(-RADIUS, RADIUS)] for k in range(3)]
        zero = jnp.zeros((8, N), jnp.float32)
        plain = [zero] * 3
        running = [zero] * 3
        for z in range(begin, end):
            for k in range(3):
                window[k] = window[k] + [plane(k, z + RADIUS, rows)]
            m = misfit[z // HALF][z % HALF, rows]
            w = window[0]
            grads = [(w[4] - w[2]) + slope[2] * (w[5] - w[1]) + slope[3] * (w[6] - w[0])]
            for k in (1, 2):
                w = window[k]
                grads.append(
                    w[3]
                    + smooth[1] * (w[4] + w[2])
                    + smooth[2] * (w[5] + w[1])
                    + smooth[3] * (w[6] + w[0])
                )
            for k in range(3):
                plain[k] = plain[k] + grads[k] * m
                running[k] = running[k] + plain[k]
                window[k] = window[k][1:]
        return plain, [plain[k] * ((end + 0.5) / E) - running[k] * (1.0 / E) for k in range(3)]

    def rows_of(r, carry):
        rows = pl.ds(pl.multiple_of(r * 8, 8), 8)
        ey = r // (E // 8)
        parts = [planes_of(rows, begin, end) for begin, end in ranges]
        row = lax.broadcasted_iota(jnp.int32, (8, N), 0) + (r % (E // 8)) * 8
        py = (row.astype(jnp.float32) + 0.5) * (1.0 / E)
        for k in range(3):
            plain = sum(p[0][k] for p in parts[1:]) + parts[0][0][k]
            upper = sum(p[1][k] for p in parts[1:]) + parts[0][1][k]
            for iz, part in enumerate((plain - upper, upper)):
                right = part * py
                sums[ey, iz * 3 + k] += part - right
                sums[ey + 1, iz * 3 + k] += right
        return carry

    lax.fori_loop(0, N // 8, rows_of, 0)


def inner_kernel(
    place, warp_a, warp_b, b2, b3, y_a, misfit_a, x_bands, y_bands, residual_in,
    residual, y, misfit, sums, rounded, sem,
):
    me, odd = place[0], place[1]
    out = filter_half(
        (2, 3), place, warp_a, warp_b, (b2, b3), x_bands, y_bands,
        residual, y, misfit, rounded, sem,
    )
    sums[...] = jnp.zeros_like(sums)
    inner = (None, [(RADIUS, E - RADIUS)])
    pl.when(me < 2)(lambda: add_up(sums, odd, (y_a, y), (misfit_a, misfit), *inner))
    pl.when(me >= 2)(lambda: add_up(sums, odd, (y, y_a), (misfit, misfit_a), *inner))
    out.wait()


def outer_kernel(
    place, edge_a, edge_b, y_a, misfit_a, y_b, misfit_b, earlier, x_bands, y_bands, hats,
    bottom, top, edges, sums,
):
    me, odd = place[0], place[1]
    planes = [edge[i] for edge in (edge_a, edge_b) for i in range(RADIUS)]
    filter_into(edges, planes, 0, x_bands, y_bands)
    sums[...] = earlier[...]

    outer = (edges, [(0, RADIUS), (E - RADIUS, E)])
    pl.when(me < 2)(lambda: add_up(sums, odd, (y_a, y_b), (misfit_a, misfit_b), *outer))
    pl.when(me >= 2)(lambda: add_up(sums, odd, (y_b, y_a), (misfit_b, misfit_a), *outer))
    out = jnp.zeros((48, N), jnp.float32)
    for iy in range(ROW + 1):
        rest = sums[iy].reshape(48, N)
        for piece in range(3):
            part = rest.astype(jnp.bfloat16)
            rest = rest - part.astype(jnp.float32)
            out = out + jnp.dot(part, hats[iy], preferred_element_type=jnp.float32)
    out = jnp.sum(out.reshape(6, 8, N), axis=1)
    for k in range(3):
        gain = float(SLOPE[RADIUS + 1] if k == 0 else SMOOTH[RADIUS]) / E
        bottom[k] = out[k : k + 1, : (ROW + 1) ** 2] * gain
        top[k] = out[3 + k : 4 + k, : (ROW + 1) ** 2] * gain


SUMS = jax.ShapeDtypeStruct((ROW + 1, 6, 8, N), jnp.float32)


def inner(place, halves, blocks, lower, residual):
    return call(
        inner_kernel,
        "inner",
        (RESIDUAL, FILTERED, HALF_VOLUME, SUMS),
        [place],
        [*halves, *blocks, *lower, *bands()],
        ROUNDED,
        32,
        hbm=[residual],
        hbm_outs=(0,),
        alias={9: 0},
    )


def assemble(place, edges, halves, earlier):
    return call(
        outer_kernel,
        "outer",
        (SMALL, SMALL),
        [place],
        [
            *edges, *halves, earlier,
            *bands(),
            jnp.asarray(RHS_HATS, jnp.bfloat16),
        ],
        [
            pltpu.VMEM((3, 2 * RADIUS, N, N), jnp.float32),
            pltpu.VMEM(SUMS.shape, jnp.float32),
        ],
        24,
    )


def body(tomogram, deformed, subvoxel, offsets):
    bricks = lax.axis_size("brick")
    me = lax.axis_index("scan")
    odd = lax.axis_index("brick") % 2
    place = jnp.stack([me, odd]).astype(jnp.int32)
    up = [(i, i + 1) for i in range(bricks - 1)]
    inside = [r for i in range(0, bricks - 1, 2) for r in ((i, i + 1), (i + 1, i))]
    outside = [r for i in range(1, bricks - 1, 2) for r in ((i, i + 1), (i + 1, i))]
    pairs = [(0, 1), (1, 0), (2, 3), (3, 2)]

    slab = pltpu.with_memory_space_constraint(deformed, pltpu.HBM)
    across = lax.ppermute(tomogram, "scan", [(0, 2), (1, 3), (2, 0), (3, 1)])
    near, far, far_end = split(place, pltpu.with_memory_space_constraint(subvoxel, pltpu.HBM), slab)
    offs = pltpu.with_memory_space_constraint(offsets.reshape(3, 1, -1), pltpu.HBM)
    halo_a = lax.ppermute(near, "brick", inside)
    halo_b = lax.ppermute(far, "brick", outside)
    halo_c = lax.ppermute(far_end, "brick", outside)
    late = tomogram
    beside = lax.ppermute(late, "scan", pairs)
    slab_parts = (near, far, far_end)
    samples = windows(place, offs, (*slab_parts, halo_a))
    across, samples = lax.optimization_barrier((across, samples))
    relayed = lax.ppermute(across, "scan", pairs)
    blocks = (tomogram, beside, across, relayed)
    warp_a, *field = first_half(place, (near, halo_a, halo_b), samples)
    warp_b, residual, *lower = second_half(
        place, offs, (*slab_parts, halo_b, halo_c, *field), warp_a, blocks[:2]
    )
    halves = (warp_a, warp_b)

    def pick(index, part):
        out = part(blocks[0])
        for j in range(1, 4):
            out = jnp.where((me ^ j) == index, part(blocks[j]), out)
        return out

    tail, head = pick(3, lambda b: b[-RADIUS:]), pick(0, lambda b: b[:RADIUS])
    send_a, send_b, lower[0] = lax.optimization_barrier(
        (jnp.where(odd == 1, head, tail), jnp.where(odd == 1, tail, head), lower[0])
    )
    edges = (lax.ppermute(send_a, "brick", inside), lax.ppermute(send_b, "brick", outside))
    residual, y, misfit, sums = inner(place, halves, blocks[2:], lower, residual)
    bottom, top = assemble(place, edges, (*lower, y, misfit), sums)
    node_rhs = bottom + lax.ppermute(top, "brick", up)
    return residual[None], node_rhs[None]


def solution(mesh):
    return jax.shard_map(
        body,
        mesh=mesh,
        in_specs=(
            P(("brick", "scan"), None, None),
            P("scan", "brick", None, None),
            P("scan", None, "brick", None),
            P("scan", None, "brick"),
        ),
        out_specs=(P("scan", "brick", None, None), P("scan", None, "brick", None)),
        check_vma=False,
    )
```

```python
import functools

import jax
import jax.numpy as jnp
import numpy as np
from jax import lax
from jax.experimental import pallas as pl
from jax.experimental.pallas import tpu as pltpu
from jax.sharding import PartitionSpec as P

E = 32
HALO = 16
RADIUS = 3
N = 128
ROW = N // E
WIN = 48
HALF = E // 2
FAR = HALO // 2
ROWS = HALO + N + E


def taps():
    t = np.arange(-RADIUS, RADIUS + 1).astype(np.float32)
    g = np.exp(-t * t / np.float32(2.0))
    smooth = g / np.sum(g)
    slope = t * g / np.sum(t * t * g)
    return [np.asarray(v, jnp.bfloat16).astype(np.float32) for v in (smooth, slope)]


def band(coeff):
    out = np.zeros((N, N), np.float32)
    for tap in range(2 * RADIUS + 1):
        out += coeff[tap] * np.eye(N, k=RADIUS - tap, dtype=np.float32)
    return out


SMOOTH, SLOPE = taps()
BAND_S, BAND_D = band(SMOOTH), band(SLOPE)
X_BANDS = np.concatenate(
    [
        np.concatenate([BAND_S, BAND_D], axis=1),
        np.concatenate([BAND_S, 0 * BAND_S], axis=1),
        np.concatenate([0 * BAND_S, BAND_S], axis=1),
    ]
)
Y_BANDS = np.concatenate([BAND_S.T, BAND_D.T], axis=0)


def rhs_hats():
    at = (np.arange(N, dtype=np.float32) + 0.5) / E
    hats = np.maximum(0.0, 1.0 - np.abs(at[:, None] - np.arange(ROW + 1, dtype=np.float32)))
    out = np.zeros((ROW + 1, N, N), np.float32)
    for iy in range(ROW + 1):
        out[iy, :, iy * (ROW + 1) : (iy + 1) * (ROW + 1)] = hats
    return out


RHS_HATS = rhs_hats()


def position():
    return lax.axis_index("scan"), lax.axis_index("brick") % 2


def lane_position(shape, dim):
    v = lax.broadcasted_iota(jnp.int32, shape, dim)
    return ((v % E).astype(jnp.float32) + 0.5) * (1.0 / E)


def split_kernel(nodes_in, slab, near, far, far_end, nodes, wide, sems):
    odd = position()[1]
    parts = ((1 - odd, 0, HALO, near), (odd, 0, FAR, far), (odd, FAR, HALO - FAR, far_end))
    copies = [
        pltpu.make_async_copy(
            slab.at[0, pl.ds(HALO * first + skip, count)], out.at[pl.ds(0, count)], sems.at[i]
        )
        for i, (first, skip, count, out) in enumerate(parts)
    ]
    fetch = pltpu.make_async_copy(nodes_in, nodes, sems.at[len(parts)])
    fetch.start()
    for c in copies:
        c.start()
    fetch.wait()
    wide[...] = jnp.zeros_like(wide)
    for c in range(3):
        wide[c : c + 1, 0 : (ROW + 1) ** 2] = nodes[0, c]
    rest = wide[...]
    rows = []
    for _ in range(3):
        rows.append(rest.astype(jnp.bfloat16).astype(jnp.float32))
        rest = rest - rows[-1]
    rows = jnp.concatenate(rows + [rest], axis=0).astype(jnp.bfloat16)
    for out, last in ((near, HALO), (far, FAR)):
        out[last, 0 : 4 * 8] = rows
        out[last, 4 * 8 : N] = jnp.zeros((N - 4 * 8, N), jnp.bfloat16)
    for c in copies:
        c.wait()


def shifted(below, offs, fetch, middle, other, halo, vol, lhs, s_val, s_dif, done=None):
    zero_top = jnp.zeros((HALO, N), jnp.float32)
    zero_end = jnp.zeros((E, N), jnp.float32)

    def fill(srcs, first):
        counts = (HALO,) if len(srcs) == 1 else (FAR, HALO - FAR)
        for src, count in zip(srcs, counts):

            def step(i, c, src=src, at=first):
                vol[at + i, 0:HALO] = zero_top
                vol[at + i, HALO : HALO + N] = src[i].astype(jnp.float32)
                vol[at + i, HALO + N : ROWS] = zero_end
                return c

            lax.fori_loop(0, count, step, 0, unroll=count // 2)
            first = first + count

    fill(halo, jnp.where(below, 0, E))
    fill(middle, HALO)
    fill(other, jnp.where(below, E, 0))
    fetch.wait()

    lane = lax.broadcasted_iota(jnp.int32, (WIN, N), 1)
    src_lane = lax.broadcasted_iota(jnp.int32, (N, N), 0)
    out_lane = lax.broadcasted_iota(jnp.int32, (N, N), 1)
    distance = src_lane - out_lane
    block = out_lane // E

    def element_row(ey):
        first_z, first_y, shift = [], [], []
        for ex in range(ROW):
            e = ey * ROW + ex
            first_z.append(offs[0, 0, e] + HALO)
            first_y.append(ey * E + offs[1, 0, e] + HALO)
            shift.append(offs[2, 0, e])
        mats = []
        for ex in range(2):
            moved = jnp.where(block == ex, distance - shift[ex], N)
            moved = jnp.where(block == ex + 2, distance - shift[ex + 2], moved)
            here = jnp.where(moved == 0, 1.0, 0.0)
            mats.append(jnp.concatenate([here, jnp.where(moved == 1, 1.0, 0.0) - here], axis=1))
        select = jnp.concatenate(mats, axis=0).astype(jnp.bfloat16)

        for z in range(HALF + 1):
            part = [vol[first_z[ex] + z, pl.ds(first_y[ex], WIN), :] for ex in range(ROW)]
            lhs[z, :, :N] = jnp.where(lane < E + HALO, part[0], part[2]).astype(jnp.bfloat16)
            lhs[z, :, N:] = jnp.where(lane < 2 * E + HALO, part[1], part[3]).astype(jnp.bfloat16)

        out = jnp.dot(
            lhs[...].reshape((HALF + 1) * WIN, 2 * N), select, preferred_element_type=jnp.float32
        )
        out = out.reshape(HALF + 1, WIN, 2 * N)
        s_val[ey] = out[:, : E + 8, :N]
        s_dif[ey] = out[:, : E + 8, N:]
        if done is not None:
            done(ey)

    for ey in range(ROW):
        element_row(ey)


def node_rows(plane, hats):
    row = lax.broadcasted_iota(jnp.int32, (16, N), 0)
    mine = lax.broadcasted_iota(jnp.int32, (16, N), 1) // (ROW + 1) == row % (ROW + 1)
    component = row // (ROW + 1)
    out = jnp.zeros((16, N), jnp.float32)
    values = plane[0 : 4 * 8].astype(jnp.float32)
    for piece in range(3):
        v = values[piece * 8 : piece * 8 + 8]
        line = jnp.where(component == 0, v[0:1], jnp.where(component == 1, v[1:2], v[2:3]))
        line = jnp.where(mine, line, 0.0).astype(jnp.bfloat16)
        out = out + jnp.dot(line, hats, preferred_element_type=jnp.float32)
    return out


def displacements(odd, near, near_halo, far_halo, w_base, w_step):
    node = lax.broadcasted_iota(jnp.int32, (N, N), 0)
    at = (lax.broadcasted_iota(jnp.int32, (N, N), 1).astype(jnp.float32) + 0.5) * (1.0 / E)
    hat = jnp.maximum(0.0, 1.0 - jnp.abs(at - (node % (ROW + 1)).astype(jnp.float32)))
    hats = jnp.where(node < (ROW + 1) ** 2, hat, 0.0).astype(jnp.bfloat16)
    lower = node_rows(near[HALO], hats)
    upper = node_rows(jnp.where(odd, far_halo[FAR], near_halo[HALO]), hats)
    py = lane_position((E, N), 0)
    for c in range(3):
        for ey in range(ROW):
            q = c * (ROW + 1) + ey
            lo = lower[q : q + 1] + py * (lower[q + 1 : q + 2] - lower[q : q + 1])
            up = upper[q : q + 1] + py * (upper[q + 1 : q + 2] - upper[q : q + 1])
            w_step[c, ey * E : (ey + 1) * E] = up - lo
            w_base[c, ey * E : (ey + 1) * E] = lo


def interpolate(val, dif, w_base, w_step, first_plane, warped, ey):
    start = first_plane.astype(jnp.float32) * (1.0 / E)

    for base in range(0, E, 8):
        at = ey * E + base
        wz1, wy1, wx1 = [w_step[k, pl.ds(at, 8)] for k in range(3)]
        wz0, wy0, wx0 = [
            w_base[k, pl.ds(at, 8)] + start * w for k, w in enumerate((wz1, wy1, wx1))
        ]

        def corners(z, base=base):
            return (
                val[ey, z, pl.ds(base, 8)],
                dif[ey, z, pl.ds(base, 8)],
                val[ey, z, pl.ds(base + 1, 8)],
                dif[ey, z, pl.ds(base + 1, 8)],
            )

        lower = corners(0)
        for z in range(HALF):
            upper = corners(z + 1)
            p = (z + 0.5) / E
            wz = wz0 + p * wz1
            wy = wy0 + p * wy1
            wx = wx0 + p * wx1
            lines = []
            for v0, d0, v1, d1 in (lower, upper):
                a0 = v0 + wx * d0
                a1 = v1 + wx * d1
                lines.append(a0 + wy * (a1 - a0))
            warped[z, pl.ds(at, 8)] = lines[0] + wz * (lines[1] - lines[0])
            lower = upper


def window_kernel(
    near, far, far_end, near_halo, offs_in,
    val_out, dif_out, vol, lhs, s_val, s_dif, offs, sem, sems,
):
    fetch = pltpu.make_async_copy(offs_in, offs, sem)
    fetch.start()

    def copies(ey):
        return [
            pltpu.make_async_copy(src.at[ey], out.at[ey], sems.at[i, ey])
            for i, (src, out) in enumerate(((s_val, val_out), (s_dif, dif_out)))
        ]

    def done(ey):
        for c in copies(ey):
            c.start()

    shifted(
        position()[1] == 1, offs, fetch, (near,), (far, far_end), (near_halo,), vol, lhs, s_val, s_dif, done
    )
    for ey in range(ROW):
        for c in copies(ey):
            c.wait()


def first_kernel(
    near, near_halo, far_halo, val_in, dif_in, warped, w_base, w_step, val, dif, sems
):
    copies = [
        [
            pltpu.make_async_copy(src.at[ey], out.at[ey], sems.at[i, ey])
            for i, (src, out) in enumerate(((val_in, val), (dif_in, dif)))
        ]
        for ey in range(ROW)
    ]
    for pair in copies:
        for c in pair:
            c.start()
    odd = position()[1] == 1
    displacements(odd, near, near_halo, far_halo, w_base, w_step)
    for ey, pair in enumerate(copies):
        for c in pair:
            c.wait()
        interpolate(val, dif, w_base, w_step, jnp.where(odd, 0, HALF), warped, ey)


def second_kernel(
    near, far, far_end, far_halo, far_halo_end, w_base, w_step,
    warp_a, b0, b1, x_bands, y_bands, offs_in,
    warped, residual, y, misfit, vol, lhs, s_val, s_dif, offs, sem, rounded, out_sem,
):
    odd = position()[1] == 1
    fetch = pltpu.make_async_copy(offs_in, offs, sem)
    fetch.start()
    halo = (far_halo, far_halo_end)
    shifted(
        jnp.logical_not(odd), offs, fetch, (far, far_end), (near,), halo, vol, lhs, s_val, s_dif
    )
    for ey in range(ROW):
        interpolate(s_val, s_dif, w_base, w_step, jnp.where(odd, HALF, 0), warped, ey)
    filter_half(
        (0, 1), warp_a, warped, (b0, b1), x_bands, y_bands,
        residual, y, misfit, rounded, out_sem,
    ).wait()


VMEM = pl.BlockSpec(memory_space=pltpu.VMEM)
HBM = pl.BlockSpec(memory_space=pltpu.HBM)
FIELD = jax.ShapeDtypeStruct((3, N, N), jnp.float32)
HALF_VOLUME = jax.ShapeDtypeStruct((HALF, N, N), jnp.float32)
SAMPLES = (ROW, HALF + 1, E + 8, N)
RESIDUAL = jax.ShapeDtypeStruct((E, N, N), jnp.bfloat16)
FILTERED = jax.ShapeDtypeStruct((3, HALF, N, N), jnp.float32)
SMALL = jax.ShapeDtypeStruct((3, 1, (ROW + 1) ** 2), jnp.float32)


def call(kernel, name, outs, vmem, scratch, mib, hbm=(), hbm_outs=(), alias=None):
    specs = [VMEM] * len(vmem)
    return pl.pallas_call(
        kernel,
        out_shape=outs,
        in_specs=specs + [HBM] * len(hbm),
        out_specs=tuple(HBM if i in hbm_outs else VMEM for i in range(len(outs))),
        input_output_aliases=alias or {},
        scratch_shapes=scratch,
        compiler_params=pltpu.CompilerParams(vmem_limit_bytes=mib * 1024 * 1024),
        name=name,
    )(*vmem, *hbm)


def split(nodes, slab):
    return call(
        split_kernel,
        "split",
        tuple(jax.ShapeDtypeStruct((n, N, N), jnp.bfloat16) for n in (HALO + 1, FAR + 1, HALO - FAR)),
        [],
        [
            pltpu.VMEM((1, 3, 1, (ROW + 1) ** 2), jnp.float32),
            pltpu.VMEM((8, N), jnp.float32),
            pltpu.SemaphoreType.DMA((4,)),
        ],
        4,
        hbm=[nodes, slab],
    )


SAMPLE_SCRATCH = [pltpu.VMEM(SAMPLES, jnp.float32)] * 2
WINDOW_SCRATCH = [
    pltpu.VMEM((E + HALO, ROWS, N), jnp.float32),
    pltpu.VMEM((HALF + 1, WIN, 2 * N), jnp.bfloat16),
    *SAMPLE_SCRATCH,
    pltpu.SMEM((3, 1, ROW * ROW), jnp.int32),
    pltpu.SemaphoreType.DMA,
]
EACH_ROW = pltpu.SemaphoreType.DMA((2, ROW))


def windows(offs, planes):
    out = pltpu.HBM(SAMPLES, jnp.float32)
    scratch = WINDOW_SCRATCH + [EACH_ROW]
    return call(
        window_kernel, "windows", (out, out), planes, scratch, 20, hbm=[offs], hbm_outs=(0, 1)
    )


def first_half(planes, samples):
    samples = [pltpu.with_memory_space_constraint(x, pltpu.HBM) for x in samples]
    scratch = SAMPLE_SCRATCH + [EACH_ROW]
    outs = (HALF_VOLUME, FIELD, FIELD)
    return call(first_kernel, "first_half", outs, planes, scratch, 16, hbm=samples)


ROUNDED = [pltpu.VMEM((HALF, N, N), jnp.bfloat16), pltpu.SemaphoreType.DMA]


def bands():
    return jnp.asarray(X_BANDS, jnp.bfloat16), jnp.asarray(Y_BANDS, jnp.bfloat16)


def second_half(offs, planes, warp_a, blocks):
    return call(
        second_kernel,
        "second_half",
        (HALF_VOLUME, RESIDUAL, FILTERED, HALF_VOLUME),
        [*planes, warp_a, *blocks, *bands()],
        WINDOW_SCRATCH + ROUNDED,
        32,
        hbm=[offs],
        hbm_outs=(1,),
    )


def filter_into(y, planes, at, x_bands, y_bands):
    count = len(planes)
    smoothed, slopes = [], []
    for i in range(0, count, 2):
        pair = jnp.concatenate(planes[i : i + 2], axis=1)
        along_y = jnp.dot(y_bands[...], pair, preferred_element_type=jnp.float32)
        along_y = along_y.astype(jnp.bfloat16)
        smoothed += [along_y[:N, :N], along_y[:N, N:]]
        slopes.append(along_y[N:])
    rows = pl.ds(at, count)
    out = jnp.dot(jnp.concatenate(smoothed), x_bands[0:N], preferred_element_type=jnp.float32)
    y[0, rows] = out[:, :N].reshape(-1, N, N)
    y[2, rows] = out[:, N:].reshape(-1, N, N)
    out = jnp.dot(jnp.concatenate(slopes), x_bands[N:], preferred_element_type=jnp.float32)
    for i in range(count):
        y[1, at + i] = out[i // 2 * N : i // 2 * N + N, i % 2 * N : i % 2 * N + N]


def filter_half(
    slots, warp_a, warp_b, blocks, x_bands, y_bands, residual, y, misfit, rounded, sem
):
    me, odd = position()
    depth = blocks[0].shape[0]
    half = (me ^ slots[0]) // 2

    def subtract(warped):
        for j, b in zip(slots, blocks):
            at = ((me ^ j) % 2) * depth
            for i in range(depth):
                m = warped[at + i] - b[i].astype(jnp.float32)
                misfit[at + i] = m
                rounded[at + i] = m.astype(jnp.bfloat16)

    pl.when(half + odd == 1)(lambda: subtract(warp_a))
    pl.when(half + odd != 1)(lambda: subtract(warp_b))
    out = pltpu.make_async_copy(rounded, residual.at[pl.ds(half * HALF, HALF)], sem)
    out.start()
    for j, b in zip(slots, blocks):
        at = ((me ^ j) % 2) * depth
        filter_into(y, [b[i] for i in range(depth)], at, x_bands, y_bands)
    return out


def add_up(sums, odd, y, misfit, edges, ranges):
    smooth = [float(SMOOTH[RADIUS + t] / SMOOTH[RADIUS]) for t in range(RADIUS + 1)]
    slope = [float(SLOPE[RADIUS + t] / SLOPE[RADIUS + 1]) for t in range(RADIUS + 1)]
    below = RADIUS * (1 - odd)
    above = RADIUS * odd

    def plane(k, z, rows):
        if z < 0:
            return edges[k, below + RADIUS + z, rows]
        if z >= E:
            return edges[k, above + z - E, rows]
        return y[z // HALF][k, z % HALF, rows]

    def planes_of(rows, begin, end):
        window = [[plane(k, begin + t, rows) for t in range(-RADIUS, RADIUS)] for k in range(3)]
        zero = jnp.zeros((8, N), jnp.float32)
        plain = [zero] * 3
        running = [zero] * 3
        for z in range(begin, end):
            for k in range(3):
                window[k] = window[k] + [plane(k, z + RADIUS, rows)]
            m = misfit[z // HALF][z % HALF, rows]
            w = window[0]
            grads = [(w[4] - w[2]) + slope[2] * (w[5] - w[1]) + slope[3] * (w[6] - w[0])]
            for k in (1, 2):
                w = window[k]
                grads.append(
                    w[3]
                    + smooth[1] * (w[4] + w[2])
                    + smooth[2] * (w[5] + w[1])
                    + smooth[3] * (w[6] + w[0])
                )
            for k in range(3):
                plain[k] = plain[k] + grads[k] * m
                running[k] = running[k] + plain[k]
                window[k] = window[k][1:]
        return plain, [plain[k] * ((end + 0.5) / E) - running[k] * (1.0 / E) for k in range(3)]

    def rows_of(r, carry):
        rows = pl.ds(pl.multiple_of(r * 8, 8), 8)
        ey = r // (E // 8)
        parts = [planes_of(rows, begin, end) for begin, end in ranges]
        row = lax.broadcasted_iota(jnp.int32, (8, N), 0) + (r % (E // 8)) * 8
        py = (row.astype(jnp.float32) + 0.5) * (1.0 / E)
        for k in range(3):
            plain = sum(p[0][k] for p in parts[1:]) + parts[0][0][k]
            upper = sum(p[1][k] for p in parts[1:]) + parts[0][1][k]
            for iz, part in enumerate((plain - upper, upper)):
                right = part * py
                sums[ey, iz * 3 + k] += part - right
                sums[ey + 1, iz * 3 + k] += right
        return carry

    lax.fori_loop(0, N // 8, rows_of, 0)


def inner_kernel(
    warp_a, warp_b, b2, b3, y_a, misfit_a, x_bands, y_bands, residual_in,
    residual, y, misfit, sums, rounded, sem,
):
    me, odd = position()
    out = filter_half(
        (2, 3), warp_a, warp_b, (b2, b3), x_bands, y_bands,
        residual, y, misfit, rounded, sem,
    )
    sums[...] = jnp.zeros_like(sums)
    inner = (None, [(RADIUS, E - RADIUS)])
    pl.when(me < 2)(lambda: add_up(sums, odd, (y_a, y), (misfit_a, misfit), *inner))
    pl.when(me >= 2)(lambda: add_up(sums, odd, (y, y_a), (misfit, misfit_a), *inner))
    out.wait()


def outer_kernel(
    edge_a, edge_b, y_a, misfit_a, y_b, misfit_b, earlier, x_bands, y_bands, hats,
    bottom, top, edges, sums,
):
    me, odd = position()
    planes = [edge[i] for edge in (edge_a, edge_b) for i in range(RADIUS)]
    filter_into(edges, planes, 0, x_bands, y_bands)
    sums[...] = earlier[...]

    outer = (edges, [(0, RADIUS), (E - RADIUS, E)])
    pl.when(me < 2)(lambda: add_up(sums, odd, (y_a, y_b), (misfit_a, misfit_b), *outer))
    pl.when(me >= 2)(lambda: add_up(sums, odd, (y_b, y_a), (misfit_b, misfit_a), *outer))
    pieces = []
    for iy in range(ROW + 1):
        rest = sums[iy].reshape(48, N)
        three = []
        for _ in range(3):
            three.append(rest.astype(jnp.bfloat16))
            rest = rest - three[-1].astype(jnp.float32)
        pieces.append(jnp.concatenate(three))
    out = jnp.dot(
        jnp.concatenate(pieces, axis=1), hats[...], preferred_element_type=jnp.float32
    )
    out = out[:48] + out[48:96] + out[96:]
    out = jnp.sum(out.reshape(6, 8, N), axis=1)
    for k in range(3):
        gain = float(SLOPE[RADIUS + 1] if k == 0 else SMOOTH[RADIUS]) / E
        bottom[k] = out[k : k + 1, : (ROW + 1) ** 2] * gain
        top[k] = out[3 + k : 4 + k, : (ROW + 1) ** 2] * gain


SUMS = jax.ShapeDtypeStruct((ROW + 1, 6, 8, N), jnp.float32)


def inner(halves, blocks, lower, residual):
    return call(
        inner_kernel,
        "inner",
        (RESIDUAL, FILTERED, HALF_VOLUME, SUMS),
        [*halves, *blocks, *lower, *bands()],
        ROUNDED,
        32,
        hbm=[residual],
        hbm_outs=(0,),
        alias={8: 0},
    )


def assemble(edges, halves, earlier):
    return call(
        outer_kernel,
        "outer",
        (SMALL, SMALL),
        [
            *edges, *halves, earlier,
            *bands(),
            jnp.asarray(RHS_HATS.reshape(-1, N), jnp.bfloat16),
        ],
        [
            pltpu.VMEM((3, 2 * RADIUS, N, N), jnp.float32),
            pltpu.VMEM(SUMS.shape, jnp.float32),
        ],
        24,
    )


def body(tomogram, deformed, subvoxel, offsets):
    bricks = lax.axis_size("brick")
    me = lax.axis_index("scan")
    odd = lax.axis_index("brick") % 2
    up = [(i, i + 1) for i in range(bricks - 1)]
    inside = [r for i in range(0, bricks - 1, 2) for r in ((i, i + 1), (i + 1, i))]
    outside = [r for i in range(1, bricks - 1, 2) for r in ((i, i + 1), (i + 1, i))]
    pairs = [(0, 1), (1, 0), (2, 3), (3, 2)]

    slab = pltpu.with_memory_space_constraint(deformed, pltpu.HBM)
    across = lax.ppermute(tomogram, "scan", [(0, 2), (1, 3), (2, 0), (3, 1)])
    near, far, far_end = split(pltpu.with_memory_space_constraint(subvoxel, pltpu.HBM), slab)
    offs = pltpu.with_memory_space_constraint(offsets.reshape(3, 1, -1), pltpu.HBM)
    halo_a = lax.ppermute(near, "brick", inside)
    halo_b = lax.ppermute(far, "brick", outside)
    halo_c = lax.ppermute(far_end, "brick", outside)
    late = tomogram
    beside = lax.ppermute(late, "scan", pairs)
    slab_parts = (near, far, far_end)
    samples = windows(offs, (*slab_parts, halo_a))
    across, samples = lax.optimization_barrier((across, samples))
    relayed = lax.ppermute(across, "scan", pairs)
    blocks = (tomogram, beside, across, relayed)
    warp_a, *field = first_half((near, halo_a, halo_b), samples)
    warp_b, residual, *lower = second_half(
        offs, (*slab_parts, halo_b, halo_c, *field), warp_a, blocks[:2]
    )
    halves = (warp_a, warp_b)

    def pick(index, part):
        out = part(blocks[0])
        for j in range(1, 4):
            out = jnp.where((me ^ j) == index, part(blocks[j]), out)
        return out

    tail, head = pick(3, lambda b: b[-RADIUS:]), pick(0, lambda b: b[:RADIUS])
    send_a, send_b, lower[0] = lax.optimization_barrier(
        (jnp.where(odd == 1, head, tail), jnp.where(odd == 1, tail, head), lower[0])
    )
    edges = (lax.ppermute(send_a, "brick", inside), lax.ppermute(send_b, "brick", outside))
    residual, y, misfit, sums = inner(halves, blocks[2:], lower, residual)
    bottom, top = assemble(edges, (*lower, y, misfit), sums)
    node_rhs = bottom + lax.ppermute(top, "brick", up)
    return residual[None], node_rhs[None]


def solution(mesh):
    return jax.shard_map(
        body,
        mesh=mesh,
        in_specs=(
            P(("brick", "scan"), None, None),
            P("scan", "brick", None, None),
            P("scan", None, "brick", None),
            P("scan", None, "brick"),
        ),
        out_specs=(P("scan", "brick", None, None), P("scan", None, "brick", None)),
        check_vma=False,
    )
```

```python
import functools

import jax
import jax.numpy as jnp
import numpy as np
from jax import lax
from jax.experimental import pallas as pl
from jax.experimental.pallas import tpu as pltpu
from jax.sharding import PartitionSpec as P

E = 32
HALO = 16
RADIUS = 3
N = 128
ROW = N // E
WIN = 48
HALF = E // 2
FAR = HALO // 2
ROWS = HALO + N + E


def taps():
    t = np.arange(-RADIUS, RADIUS + 1).astype(np.float32)
    g = np.exp(-t * t / np.float32(2.0))
    smooth = g / np.sum(g)
    slope = t * g / np.sum(t * t * g)
    return [np.asarray(v, jnp.bfloat16).astype(np.float32) for v in (smooth, slope)]


def band(coeff):
    out = np.zeros((N, N), np.float32)
    for tap in range(2 * RADIUS + 1):
        out += coeff[tap] * np.eye(N, k=RADIUS - tap, dtype=np.float32)
    return out


SMOOTH, SLOPE = taps()
BAND_S, BAND_D = band(SMOOTH), band(SLOPE)
X_BANDS = np.concatenate(
    [
        np.concatenate([BAND_S, BAND_D], axis=1),
        np.concatenate([BAND_S, 0 * BAND_S], axis=1),
        np.concatenate([0 * BAND_S, BAND_S], axis=1),
    ]
)
Y_BANDS = np.concatenate([BAND_S.T, BAND_D.T], axis=0)


def rhs_hats():
    at = (np.arange(N, dtype=np.float32) + 0.5) / E
    hats = np.maximum(0.0, 1.0 - np.abs(at[:, None] - np.arange(ROW + 1, dtype=np.float32)))
    out = np.zeros((ROW + 1, N, N), np.float32)
    for iy in range(ROW + 1):
        out[iy, :, iy * (ROW + 1) : (iy + 1) * (ROW + 1)] = hats
    return out


RHS_HATS = rhs_hats()


def position():
    return lax.axis_index("scan"), lax.axis_index("brick") % 2


def lane_position(shape, dim):
    v = lax.broadcasted_iota(jnp.int32, shape, dim)
    return ((v % E).astype(jnp.float32) + 0.5) * (1.0 / E)


def split_kernel(nodes_in, slab, near, far, far_end, nodes, wide, sems):
    odd = position()[1]
    parts = ((1 - odd, 0, HALO, near), (odd, 0, FAR, far), (odd, FAR, HALO - FAR, far_end))
    copies = [
        pltpu.make_async_copy(
            slab.at[0, pl.ds(HALO * first + skip, count)], out.at[pl.ds(0, count)], sems.at[i]
        )
        for i, (first, skip, count, out) in enumerate(parts)
    ]
    fetch = pltpu.make_async_copy(nodes_in, nodes, sems.at[len(parts)])
    fetch.start()
    for c in copies:
        c.start()
    fetch.wait()
    wide[...] = jnp.zeros_like(wide)
    for c in range(3):
        wide[c : c + 1, 0 : (ROW + 1) ** 2] = nodes[0, c]
    rest = wide[...]
    rows = []
    for _ in range(3):
        rows.append(rest.astype(jnp.bfloat16).astype(jnp.float32))
        rest = rest - rows[-1]
    rows = jnp.concatenate(rows + [rest], axis=0).astype(jnp.bfloat16)
    for out, last in ((near, HALO), (far, FAR)):
        out[last, 0 : 4 * 8] = rows
        out[last, 4 * 8 : N] = jnp.zeros((N - 4 * 8, N), jnp.bfloat16)
    for c in copies:
        c.wait()


def shifted(below, offs, fetch, middle, other, halo, vol, lhs, s_val, s_dif, done=None):
    zero_top = jnp.zeros((HALO, N), jnp.float32)
    zero_end = jnp.zeros((E, N), jnp.float32)

    def fill(srcs, first):
        counts = (HALO,) if len(srcs) == 1 else (FAR, HALO - FAR)
        for src, count in zip(srcs, counts):

            def step(i, c, src=src, at=first):
                vol[at + i, 0:HALO] = zero_top
                vol[at + i, HALO : HALO + N] = src[i].astype(jnp.float32)
                vol[at + i, HALO + N : ROWS] = zero_end
                return c

            lax.fori_loop(0, count, step, 0, unroll=count // 2)
            first = first + count

    fill(halo, jnp.where(below, 0, E))
    fill(middle, HALO)
    fill(other, jnp.where(below, E, 0))
    fetch.wait()

    lane = lax.broadcasted_iota(jnp.int32, (WIN, N), 1)
    src_lane = lax.broadcasted_iota(jnp.int32, (N, N), 0)
    out_lane = lax.broadcasted_iota(jnp.int32, (N, N), 1)
    distance = src_lane - out_lane
    block = out_lane // E

    def element_row(ey):
        first_z, first_y, shift = [], [], []
        for ex in range(ROW):
            e = ey * ROW + ex
            first_z.append(offs[0, 0, e] + HALO)
            first_y.append(ey * E + offs[1, 0, e] + HALO)
            shift.append(offs[2, 0, e])
        mats = []
        for ex in range(2):
            moved = jnp.where(block == ex, distance - shift[ex], N)
            moved = jnp.where(block == ex + 2, distance - shift[ex + 2], moved)
            here = jnp.where(moved == 0, 1.0, 0.0)
            mats.append(jnp.concatenate([here, jnp.where(moved == 1, 1.0, 0.0) - here], axis=1))
        select = jnp.concatenate(mats, axis=0).astype(jnp.bfloat16)

        for z in range(HALF + 1):
            part = [vol[first_z[ex] + z, pl.ds(first_y[ex], WIN), :] for ex in range(ROW)]
            lhs[z, :, :N] = jnp.where(lane < E + HALO, part[0], part[2]).astype(jnp.bfloat16)
            lhs[z, :, N:] = jnp.where(lane < 2 * E + HALO, part[1], part[3]).astype(jnp.bfloat16)

        out = jnp.dot(
            lhs[...].reshape((HALF + 1) * WIN, 2 * N), select, preferred_element_type=jnp.float32
        )
        out = out.reshape(HALF + 1, WIN, 2 * N)
        s_val[ey] = out[:, : E + 8, :N]
        s_dif[ey] = out[:, : E + 8, N:]
        if done is not None:
            done(ey)

    for ey in range(ROW):
        element_row(ey)


def node_rows(plane, hats):
    row = lax.broadcasted_iota(jnp.int32, (16, N), 0)
    mine = lax.broadcasted_iota(jnp.int32, (16, N), 1) // (ROW + 1) == row % (ROW + 1)
    component = row // (ROW + 1)
    out = jnp.zeros((16, N), jnp.float32)
    values = plane[0 : 4 * 8].astype(jnp.float32)
    for piece in range(3):
        v = values[piece * 8 : piece * 8 + 8]
        line = jnp.where(component == 0, v[0:1], jnp.where(component == 1, v[1:2], v[2:3]))
        line = jnp.where(mine, line, 0.0).astype(jnp.bfloat16)
        out = out + jnp.dot(line, hats, preferred_element_type=jnp.float32)
    return out


def displacements(odd, near, near_halo, far_halo, w_base, w_step):
    node = lax.broadcasted_iota(jnp.int32, (N, N), 0)
    at = (lax.broadcasted_iota(jnp.int32, (N, N), 1).astype(jnp.float32) + 0.5) * (1.0 / E)
    hat = jnp.maximum(0.0, 1.0 - jnp.abs(at - (node % (ROW + 1)).astype(jnp.float32)))
    hats = jnp.where(node < (ROW + 1) ** 2, hat, 0.0).astype(jnp.bfloat16)
    lower = node_rows(near[HALO], hats)
    upper = node_rows(jnp.where(odd, far_halo[FAR], near_halo[HALO]), hats)
    py = lane_position((E, N), 0)
    for c in range(3):
        for ey in range(ROW):
            q = c * (ROW + 1) + ey
            lo = lower[q : q + 1] + py * (lower[q + 1 : q + 2] - lower[q : q + 1])
            up = upper[q : q + 1] + py * (upper[q + 1 : q + 2] - upper[q : q + 1])
            w_step[c, ey * E : (ey + 1) * E] = up - lo
            w_base[c, ey * E : (ey + 1) * E] = lo


def interpolate(val, dif, w_base, w_step, first_plane, warped, ey):
    start = first_plane.astype(jnp.float32) * (1.0 / E)

    for base in range(0, E, 8):
        at = ey * E + base
        wz1, wy1, wx1 = [w_step[k, pl.ds(at, 8)] for k in range(3)]
        wz0, wy0, wx0 = [
            w_base[k, pl.ds(at, 8)] + start * w for k, w in enumerate((wz1, wy1, wx1))
        ]

        def corners(z, base=base):
            return (
                val[ey, z, pl.ds(base, 8)],
                dif[ey, z, pl.ds(base, 8)],
                val[ey, z, pl.ds(base + 1, 8)],
                dif[ey, z, pl.ds(base + 1, 8)],
            )

        lower = corners(0)
        for z in range(HALF):
            upper = corners(z + 1)
            p = (z + 0.5) / E
            wz = wz0 + p * wz1
            wy = wy0 + p * wy1
            wx = wx0 + p * wx1
            lines = []
            for v0, d0, v1, d1 in (lower, upper):
                a0 = v0 + wx * d0
                a1 = v1 + wx * d1
                lines.append(a0 + wy * (a1 - a0))
            warped[z, pl.ds(at, 8)] = lines[0] + wz * (lines[1] - lines[0])
            lower = upper


def window_kernel(
    near, far, far_end, near_halo, offs_in,
    val_out, dif_out, vol, lhs, s_val, s_dif, offs, sem, sems,
):
    fetch = pltpu.make_async_copy(offs_in, offs, sem)
    fetch.start()

    def copies(ey):
        return [
            pltpu.make_async_copy(src.at[ey], out.at[ey], sems.at[i, ey])
            for i, (src, out) in enumerate(((s_val, val_out), (s_dif, dif_out)))
        ]

    def done(ey):
        for c in copies(ey):
            c.start()

    shifted(
        position()[1] == 1, offs, fetch, (near,), (far, far_end), (near_halo,), vol, lhs, s_val, s_dif, done
    )
    for ey in range(ROW):
        for c in copies(ey):
            c.wait()


def first_kernel(
    near, near_halo, far_halo, val_in, dif_in, warped, w_base, w_step, val, dif, sems
):
    copies = [
        [
            pltpu.make_async_copy(src.at[ey], out.at[ey], sems.at[i, ey])
            for i, (src, out) in enumerate(((val_in, val), (dif_in, dif)))
        ]
        for ey in range(ROW)
    ]
    for pair in copies:
        for c in pair:
            c.start()
    odd = position()[1] == 1
    displacements(odd, near, near_halo, far_halo, w_base, w_step)
    for ey, pair in enumerate(copies):
        for c in pair:
            c.wait()
        interpolate(val, dif, w_base, w_step, jnp.where(odd, 0, HALF), warped, ey)


def second_kernel(
    near, far, far_end, far_halo, far_halo_end, w_base, w_step,
    warp_a, b0, b1, x_bands, y_bands, offs_in,
    warped, residual, y, misfit, vol, lhs, s_val, s_dif, offs, sem, rounded, out_sem,
):
    odd = position()[1] == 1
    fetch = pltpu.make_async_copy(offs_in, offs, sem)
    fetch.start()
    halo = (far_halo, far_halo_end)
    shifted(
        jnp.logical_not(odd), offs, fetch, (far, far_end), (near,), halo, vol, lhs, s_val, s_dif
    )
    for ey in range(ROW):
        interpolate(s_val, s_dif, w_base, w_step, jnp.where(odd, HALF, 0), warped, ey)
    filter_half(
        (0, 1), warp_a, warped, (b0, b1), x_bands, y_bands,
        residual, y, misfit, rounded, out_sem,
    ).wait()


VMEM = pl.BlockSpec(memory_space=pltpu.VMEM)
HBM = pl.BlockSpec(memory_space=pltpu.HBM)
FIELD = jax.ShapeDtypeStruct((3, N, N), jnp.float32)
HALF_VOLUME = jax.ShapeDtypeStruct((HALF, N, N), jnp.float32)
SAMPLES = (ROW, HALF + 1, E + 8, N)
RESIDUAL = jax.ShapeDtypeStruct((E, N, N), jnp.bfloat16)
FILTERED = jax.ShapeDtypeStruct((3, HALF, N, N), jnp.float32)
SMALL = jax.ShapeDtypeStruct((3, 1, (ROW + 1) ** 2), jnp.float32)


def call(kernel, name, outs, vmem, scratch, mib, hbm=(), hbm_outs=(), alias=None):
    specs = [VMEM] * len(vmem)
    return pl.pallas_call(
        kernel,
        out_shape=outs,
        in_specs=specs + [HBM] * len(hbm),
        out_specs=tuple(HBM if i in hbm_outs else VMEM for i in range(len(outs))),
        input_output_aliases=alias or {},
        scratch_shapes=scratch,
        compiler_params=pltpu.CompilerParams(vmem_limit_bytes=mib * 1024 * 1024),
        name=name,
    )(*vmem, *hbm)


def split(nodes, slab):
    return call(
        split_kernel,
        "split",
        tuple(jax.ShapeDtypeStruct((n, N, N), jnp.bfloat16) for n in (HALO + 1, FAR + 1, HALO - FAR)),
        [],
        [
            pltpu.VMEM((1, 3, 1, (ROW + 1) ** 2), jnp.float32),
            pltpu.VMEM((8, N), jnp.float32),
            pltpu.SemaphoreType.DMA((4,)),
        ],
        4,
        hbm=[nodes, slab],
    )


SAMPLE_SCRATCH = [pltpu.VMEM(SAMPLES, jnp.float32)] * 2
WINDOW_SCRATCH = [
    pltpu.VMEM((E + HALO, ROWS, N), jnp.float32),
    pltpu.VMEM((HALF + 1, WIN, 2 * N), jnp.bfloat16),
    *SAMPLE_SCRATCH,
    pltpu.SMEM((3, 1, ROW * ROW), jnp.int32),
    pltpu.SemaphoreType.DMA,
]
EACH_ROW = pltpu.SemaphoreType.DMA((2, ROW))


def windows(offs, planes):
    out = pltpu.HBM(SAMPLES, jnp.float32)
    scratch = WINDOW_SCRATCH + [EACH_ROW]
    return call(
        window_kernel, "windows", (out, out), planes, scratch, 20, hbm=[offs], hbm_outs=(0, 1)
    )


def first_half(planes, samples):
    samples = [pltpu.with_memory_space_constraint(x, pltpu.HBM) for x in samples]
    scratch = SAMPLE_SCRATCH + [EACH_ROW]
    outs = (HALF_VOLUME, FIELD, FIELD)
    return call(first_kernel, "first_half", outs, planes, scratch, 16, hbm=samples)


EDGES = pltpu.VMEM((3, RADIUS + 1, N, N), jnp.float32)
ROUNDED = [pltpu.VMEM((HALF, N, N), jnp.bfloat16), pltpu.SemaphoreType.DMA]


def bands():
    return jnp.asarray(X_BANDS, jnp.bfloat16), jnp.asarray(Y_BANDS, jnp.bfloat16)


def second_half(offs, planes, warp_a, blocks):
    return call(
        second_kernel,
        "second_half",
        (HALF_VOLUME, RESIDUAL, FILTERED, HALF_VOLUME),
        [*planes, warp_a, *blocks, *bands()],
        WINDOW_SCRATCH + ROUNDED,
        32,
        hbm=[offs],
        hbm_outs=(1,),
    )


def filter_into(y, planes, at, x_bands, y_bands):
    count = len(planes)
    smoothed, slopes = [], []
    for i in range(0, count, 2):
        pair = jnp.concatenate(planes[i : i + 2], axis=1)
        along_y = jnp.dot(y_bands[...], pair, preferred_element_type=jnp.float32)
        along_y = along_y.astype(jnp.bfloat16)
        smoothed += [along_y[:N, :N], along_y[:N, N:]]
        slopes.append(along_y[N:])
    rows = pl.ds(at, count)
    out = jnp.dot(jnp.concatenate(smoothed), x_bands[0:N], preferred_element_type=jnp.float32)
    y[0, rows] = out[:, :N].reshape(-1, N, N)
    y[2, rows] = out[:, N:].reshape(-1, N, N)
    out = jnp.dot(jnp.concatenate(slopes), x_bands[N:], preferred_element_type=jnp.float32)
    for i in range(count):
        y[1, at + i] = out[i // 2 * N : i // 2 * N + N, i % 2 * N : i % 2 * N + N]


def filter_half(
    slots, warp_a, warp_b, blocks, x_bands, y_bands, residual, y, misfit, rounded, sem
):
    me, odd = position()
    depth = blocks[0].shape[0]
    half = (me ^ slots[0]) // 2

    def subtract(warped):
        for j, b in zip(slots, blocks):
            at = ((me ^ j) % 2) * depth
            for i in range(depth):
                m = warped[at + i] - b[i].astype(jnp.float32)
                misfit[at + i] = m
                rounded[at + i] = m.astype(jnp.bfloat16)

    pl.when(half + odd == 1)(lambda: subtract(warp_a))
    pl.when(half + odd != 1)(lambda: subtract(warp_b))
    out = pltpu.make_async_copy(rounded, residual.at[pl.ds(half * HALF, HALF)], sem)
    out.start()
    for j, b in zip(slots, blocks):
        at = ((me ^ j) % 2) * depth
        filter_into(y, [b[i] for i in range(depth)], at, x_bands, y_bands)
    return out


def add_up(sums, y, misfit, edges, begin, end):
    smooth = [float(SMOOTH[RADIUS + t] / SMOOTH[RADIUS]) for t in range(RADIUS + 1)]
    slope = [float(SLOPE[RADIUS + t] / SLOPE[RADIUS + 1]) for t in range(RADIUS + 1)]

    def plane(k, z, rows):
        if z < 0:
            return edges[k, RADIUS + z, rows]
        if z >= E:
            return edges[k, z - E, rows]
        return y[z // HALF][k, z % HALF, rows]

    def planes_of(rows):
        window = [[plane(k, begin + t, rows) for t in range(-RADIUS, RADIUS)] for k in range(3)]
        zero = jnp.zeros((8, N), jnp.float32)
        plain = [zero] * 3
        running = [zero] * 3
        for z in range(begin, end):
            for k in range(3):
                window[k] = window[k] + [plane(k, z + RADIUS, rows)]
            m = misfit[z // HALF][z % HALF, rows]
            w = window[0]
            grads = [(w[4] - w[2]) + slope[2] * (w[5] - w[1]) + slope[3] * (w[6] - w[0])]
            for k in (1, 2):
                w = window[k]
                grads.append(
                    w[3]
                    + smooth[1] * (w[4] + w[2])
                    + smooth[2] * (w[5] + w[1])
                    + smooth[3] * (w[6] + w[0])
                )
            for k in range(3):
                plain[k] = plain[k] + grads[k] * m
                running[k] = running[k] + plain[k]
                window[k] = window[k][1:]
        return plain, [plain[k] * ((end + 0.5) / E) - running[k] * (1.0 / E) for k in range(3)]

    def rows_of(r, carry):
        rows = pl.ds(pl.multiple_of(r * 8, 8), 8)
        ey = r // (E // 8)
        plains, uppers = planes_of(rows)
        row = lax.broadcasted_iota(jnp.int32, (8, N), 0) + (r % (E // 8)) * 8
        py = (row.astype(jnp.float32) + 0.5) * (1.0 / E)
        for k in range(3):
            for iz, part in enumerate((plains[k] - uppers[k], uppers[k])):
                right = part * py
                sums[ey, iz * 3 + k] += part - right
                sums[ey + 1, iz * 3 + k] += right
        return carry

    lax.fori_loop(0, N // 8, rows_of, 0)


def in_each_case(add, low, high, near_end):
    me, odd = position()
    for first_low in (True, False):
        for start in (True, False):
            parts = (low, high) if first_low else (high, low)
            case = ((me < 2) == first_low) & ((odd == 1) == (start == near_end))
            inner = (0, E - RADIUS) if start else (RADIUS, E)
            outer = (0, RADIUS) if start else (E - RADIUS, E)
            pl.when(case)(
                lambda parts=parts, planes=inner if near_end else outer: add(*zip(*parts), *planes)
            )


def inner_kernel(
    warp_a, warp_b, b2, b3, edge, y_a, misfit_a, x_bands, y_bands, residual_in,
    residual, y, misfit, sums, rounded, sem, edges,
):
    out = filter_half(
        (2, 3), warp_a, warp_b, (b2, b3), x_bands, y_bands,
        residual, y, misfit, rounded, sem,
    )
    sums[...] = jnp.zeros_like(sums)
    planes = [edge[i] for i in (0, 1, 2, 2)]
    filter_into(edges, planes, 0, x_bands, y_bands)
    in_each_case(
        lambda ys, misfits, begin, end: add_up(sums, ys, misfits, edges, begin, end),
        (y_a, misfit_a), (y, misfit), True,
    )
    out.wait()


def outer_kernel(
    edge, y_a, misfit_a, y_b, misfit_b, earlier, x_bands, y_bands, hats,
    bottom, top, edges, sums,
):
    planes = [edge[i] for i in (0, 1, 2, 2)]
    filter_into(edges, planes, 0, x_bands, y_bands)
    sums[...] = earlier[...]
    in_each_case(
        lambda ys, misfits, begin, end: add_up(sums, ys, misfits, edges, begin, end),
        (y_a, misfit_a), (y_b, misfit_b), False,
    )
    pieces = []
    for iy in range(ROW + 1):
        rest = sums[iy].reshape(48, N)
        three = []
        for _ in range(3):
            three.append(rest.astype(jnp.bfloat16))
            rest = rest - three[-1].astype(jnp.float32)
        pieces.append(jnp.concatenate(three))
    out = jnp.dot(
        jnp.concatenate(pieces, axis=1), hats[...], preferred_element_type=jnp.float32
    )
    out = out[:48] + out[48:96] + out[96:]
    out = jnp.sum(out.reshape(6, 8, N), axis=1)
    for k in range(3):
        gain = float(SLOPE[RADIUS + 1] if k == 0 else SMOOTH[RADIUS]) / E
        bottom[k] = out[k : k + 1, : (ROW + 1) ** 2] * gain
        top[k] = out[3 + k : 4 + k, : (ROW + 1) ** 2] * gain


SUMS = jax.ShapeDtypeStruct((ROW + 1, 6, 8, N), jnp.float32)


def inner(halves, blocks, edge, lower, residual):
    return call(
        inner_kernel,
        "inner",
        (RESIDUAL, FILTERED, HALF_VOLUME, SUMS),
        [*halves, *blocks, edge, *lower, *bands()],
        ROUNDED + [EDGES],
        32,
        hbm=[residual],
        hbm_outs=(0,),
        alias={9: 0},
    )


def assemble(edge, halves, earlier):
    return call(
        outer_kernel,
        "outer",
        (SMALL, SMALL),
        [
            edge, *halves, earlier,
            *bands(),
            jnp.asarray(RHS_HATS.reshape(-1, N), jnp.bfloat16),
        ],
        [
            EDGES,
            pltpu.VMEM(SUMS.shape, jnp.float32),
        ],
        24,
    )


def body(tomogram, deformed, subvoxel, offsets):
    bricks = lax.axis_size("brick")
    me = lax.axis_index("scan")
    odd = lax.axis_index("brick") % 2
    up = [(i, i + 1) for i in range(bricks - 1)]
    inside = [r for i in range(0, bricks - 1, 2) for r in ((i, i + 1), (i + 1, i))]
    outside = [r for i in range(1, bricks - 1, 2) for r in ((i, i + 1), (i + 1, i))]
    pairs = [(0, 1), (1, 0), (2, 3), (3, 2)]

    slab = pltpu.with_memory_space_constraint(deformed, pltpu.HBM)
    across = lax.ppermute(tomogram, "scan", [(0, 2), (1, 3), (2, 0), (3, 1)])
    near, far, far_end = split(pltpu.with_memory_space_constraint(subvoxel, pltpu.HBM), slab)
    offs = pltpu.with_memory_space_constraint(offsets.reshape(3, 1, -1), pltpu.HBM)
    halo_a = lax.ppermute(near, "brick", inside)
    halo_b = lax.ppermute(far, "brick", outside)
    halo_c = lax.ppermute(far_end, "brick", outside)
    late = tomogram
    beside = lax.ppermute(late, "scan", pairs)
    slab_parts = (near, far, far_end)
    samples = windows(offs, (*slab_parts, halo_a))
    across, samples = lax.optimization_barrier((across, samples))
    relayed = lax.ppermute(across, "scan", pairs)
    blocks = (tomogram, beside, across, relayed)
    warp_a, *field = first_half((near, halo_a, halo_b), samples)
    warp_b, residual, *lower = second_half(
        offs, (*slab_parts, halo_b, halo_c, *field), warp_a, blocks[:2]
    )
    halves = (warp_a, warp_b)

    def pick(index, part):
        out = part(blocks[0])
        for j in range(1, 4):
            out = jnp.where((me ^ j) == index, part(blocks[j]), out)
        return out

    tail, head = pick(3, lambda b: b[-RADIUS:]), pick(0, lambda b: b[:RADIUS])
    send_a, send_b, lower[0] = lax.optimization_barrier(
        (jnp.where(odd == 1, head, tail), jnp.where(odd == 1, tail, head), lower[0])
    )
    edge_a = lax.ppermute(send_a, "brick", inside)
    edge_b = lax.ppermute(send_b, "brick", outside)
    residual, y, misfit, sums = inner(halves, blocks[2:], edge_a, lower, residual)
    bottom, top = assemble(edge_b, (*lower, y, misfit), sums)
    node_rhs = bottom + lax.ppermute(top, "brick", up)
    return residual[None], node_rhs[None]


def solution(mesh):
    return jax.shard_map(
        body,
        mesh=mesh,
        in_specs=(
            P(("brick", "scan"), None, None),
            P("scan", "brick", None, None),
            P("scan", None, "brick", None),
            P("scan", None, "brick"),
        ),
        out_specs=(P("scan", "brick", None, None), P("scan", None, "brick", None)),
        check_vma=False,
    )
```

```python
import functools

import jax
import jax.numpy as jnp
import numpy as np
from jax import lax
from jax.experimental import pallas as pl
from jax.experimental.pallas import tpu as pltpu
from jax.sharding import PartitionSpec as P

E = 32
HALO = 16
RADIUS = 3
N = 128
ROW = N // E
WIN = 48
HALF = E // 2
FAR = HALO // 2
ROWS = HALO + N + E


def taps():
    t = np.arange(-RADIUS, RADIUS + 1).astype(np.float32)
    g = np.exp(-t * t / np.float32(2.0))
    smooth = g / np.sum(g)
    slope = t * g / np.sum(t * t * g)
    return [np.asarray(v, jnp.bfloat16).astype(np.float32) for v in (smooth, slope)]


def band(coeff):
    out = np.zeros((N, N), np.float32)
    for tap in range(2 * RADIUS + 1):
        out += coeff[tap] * np.eye(N, k=RADIUS - tap, dtype=np.float32)
    return out


SMOOTH, SLOPE = taps()
BAND_S, BAND_D = band(SMOOTH), band(SLOPE)
X_BANDS = np.concatenate(
    [
        np.concatenate([BAND_S, BAND_D], axis=1),
        np.concatenate([BAND_S, 0 * BAND_S], axis=1),
        np.concatenate([0 * BAND_S, BAND_S], axis=1),
    ]
)
Y_BANDS = np.concatenate([BAND_S.T, BAND_D.T], axis=0)


def rhs_hats():
    at = (np.arange(N, dtype=np.float32) + 0.5) / E
    hats = np.maximum(0.0, 1.0 - np.abs(at[:, None] - np.arange(ROW + 1, dtype=np.float32)))
    out = np.zeros((ROW + 1, N, N), np.float32)
    for iy in range(ROW + 1):
        out[iy, :, iy * (ROW + 1) : (iy + 1) * (ROW + 1)] = hats
    return out


RHS_HATS = rhs_hats()


def position():
    return lax.axis_index("scan"), lax.axis_index("brick") % 2


def lane_position(shape, dim):
    v = lax.broadcasted_iota(jnp.int32, shape, dim)
    return ((v % E).astype(jnp.float32) + 0.5) * (1.0 / E)


def split_kernel(nodes_in, slab, near, far, far_end, nodes, wide, sems):
    odd = position()[1]
    parts = ((1 - odd, 0, HALO, near), (odd, 0, FAR, far), (odd, FAR, HALO - FAR, far_end))
    copies = [
        pltpu.make_async_copy(
            slab.at[0, pl.ds(HALO * first + skip, count)], out.at[pl.ds(0, count)], sems.at[i]
        )
        for i, (first, skip, count, out) in enumerate(parts)
    ]
    fetch = pltpu.make_async_copy(nodes_in, nodes, sems.at[len(parts)])
    for c in copies:
        c.start()
    fetch.start()
    fetch.wait()
    wide[...] = jnp.zeros_like(wide)
    for c in range(3):
        wide[c : c + 1, 0 : (ROW + 1) ** 2] = nodes[0, c]
    rest = wide[...]
    rows = []
    for _ in range(3):
        rows.append(rest.astype(jnp.bfloat16).astype(jnp.float32))
        rest = rest - rows[-1]
    rows = jnp.concatenate(rows + [rest], axis=0).astype(jnp.bfloat16)
    for out, last in ((near, HALO), (far, FAR)):
        out[last, 0 : 4 * 8] = rows
        out[last, 4 * 8 : N] = jnp.zeros((N - 4 * 8, N), jnp.bfloat16)
    for c in copies:
        c.wait()


def shifted(below, offs, fetch, middle, other, halo, vol, lhs, s_val, s_dif, done=None):
    zero_top = jnp.zeros((HALO, N), jnp.float32)
    zero_end = jnp.zeros((E, N), jnp.float32)

    def fill(srcs, first):
        counts = (HALO,) if len(srcs) == 1 else (FAR, HALO - FAR)
        for src, count in zip(srcs, counts):

            def step(i, c, src=src, at=first):
                vol[at + i, 0:HALO] = zero_top
                vol[at + i, HALO : HALO + N] = src[i].astype(jnp.float32)
                vol[at + i, HALO + N : ROWS] = zero_end
                return c

            lax.fori_loop(0, count, step, 0, unroll=count // 2)
            first = first + count

    fill(halo, jnp.where(below, 0, E))
    fill(middle, HALO)
    fill(other, jnp.where(below, E, 0))
    fetch.wait()

    lane = lax.broadcasted_iota(jnp.int32, (WIN, N), 1)
    src_lane = lax.broadcasted_iota(jnp.int32, (N, N), 0)
    out_lane = lax.broadcasted_iota(jnp.int32, (N, N), 1)
    distance = src_lane - out_lane
    block = out_lane // E

    def element_row(ey):
        first_z, first_y, shift = [], [], []
        for ex in range(ROW):
            e = ey * ROW + ex
            first_z.append(offs[0, 0, e] + HALO)
            first_y.append(ey * E + offs[1, 0, e] + HALO)
            shift.append(offs[2, 0, e])
        mats = []
        for ex in range(2):
            moved = jnp.where(block == ex, distance - shift[ex], N)
            moved = jnp.where(block == ex + 2, distance - shift[ex + 2], moved)
            here = jnp.where(moved == 0, 1.0, 0.0)
            mats.append(jnp.concatenate([here, jnp.where(moved == 1, 1.0, 0.0) - here], axis=1))
        select = jnp.concatenate(mats, axis=0).astype(jnp.bfloat16)

        for z in range(HALF + 1):
            part = [vol[first_z[ex] + z, pl.ds(first_y[ex], WIN), :] for ex in range(ROW)]
            lhs[z, :, :N] = jnp.where(lane < E + HALO, part[0], part[2]).astype(jnp.bfloat16)
            lhs[z, :, N:] = jnp.where(lane < 2 * E + HALO, part[1], part[3]).astype(jnp.bfloat16)

        out = jnp.dot(
            lhs[...].reshape((HALF + 1) * WIN, 2 * N), select, preferred_element_type=jnp.float32
        )
        out = out.reshape(HALF + 1, WIN, 2 * N)
        s_val[ey] = out[:, : E + 8, :N]
        s_dif[ey] = out[:, : E + 8, N:]
        if done is not None:
            done(ey)

    for ey in range(ROW):
        element_row(ey)


def node_rows(plane, hats):
    row = lax.broadcasted_iota(jnp.int32, (16, N), 0)
    mine = lax.broadcasted_iota(jnp.int32, (16, N), 1) // (ROW + 1) == row % (ROW + 1)
    component = row // (ROW + 1)
    out = jnp.zeros((16, N), jnp.float32)
    values = plane[0 : 4 * 8].astype(jnp.float32)
    for piece in range(3):
        v = values[piece * 8 : piece * 8 + 8]
        line = jnp.where(component == 0, v[0:1], jnp.where(component == 1, v[1:2], v[2:3]))
        line = jnp.where(mine, line, 0.0).astype(jnp.bfloat16)
        out = out + jnp.dot(line, hats, preferred_element_type=jnp.float32)
    return out


def displacements(odd, near, near_halo, far_halo, w_base, w_step):
    node = lax.broadcasted_iota(jnp.int32, (N, N), 0)
    at = (lax.broadcasted_iota(jnp.int32, (N, N), 1).astype(jnp.float32) + 0.5) * (1.0 / E)
    hat = jnp.maximum(0.0, 1.0 - jnp.abs(at - (node % (ROW + 1)).astype(jnp.float32)))
    hats = jnp.where(node < (ROW + 1) ** 2, hat, 0.0).astype(jnp.bfloat16)
    lower = node_rows(near[HALO], hats)
    upper = node_rows(jnp.where(odd, far_halo[FAR], near_halo[HALO]), hats)
    py = lane_position((E, N), 0)
    for c in range(3):
        for ey in range(ROW):
            q = c * (ROW + 1) + ey
            lo = lower[q : q + 1] + py * (lower[q + 1 : q + 2] - lower[q : q + 1])
            up = upper[q : q + 1] + py * (upper[q + 1 : q + 2] - upper[q : q + 1])
            w_step[c, ey * E : (ey + 1) * E] = up - lo
            w_base[c, ey * E : (ey + 1) * E] = lo


def interpolate(val, dif, w_base, w_step, first_plane, warped, ey):
    start = first_plane.astype(jnp.float32) * (1.0 / E)

    for base in range(0, E, 8):
        at = ey * E + base
        wz1, wy1, wx1 = [w_step[k, pl.ds(at, 8)] for k in range(3)]
        wz0, wy0, wx0 = [
            w_base[k, pl.ds(at, 8)] + start * w for k, w in enumerate((wz1, wy1, wx1))
        ]

        def corners(z, base=base):
            return (
                val[ey, z, pl.ds(base, 8)],
                dif[ey, z, pl.ds(base, 8)],
                val[ey, z, pl.ds(base + 1, 8)],
                dif[ey, z, pl.ds(base + 1, 8)],
            )

        lower = corners(0)
        for z in range(HALF):
            upper = corners(z + 1)
            p = (z + 0.5) / E
            wz = wz0 + p * wz1
            wy = wy0 + p * wy1
            wx = wx0 + p * wx1
            lines = []
            for v0, d0, v1, d1 in (lower, upper):
                a0 = v0 + wx * d0
                a1 = v1 + wx * d1
                lines.append(a0 + wy * (a1 - a0))
            warped[z, pl.ds(at, 8)] = lines[0] + wz * (lines[1] - lines[0])
            lower = upper


def window_kernel(
    near, far, far_end, near_halo, offs_in,
    val_out, dif_out, vol, lhs, s_val, s_dif, offs, sem, sems,
):
    fetch = pltpu.make_async_copy(offs_in, offs, sem)
    fetch.start()

    def copies(ey):
        return [
            pltpu.make_async_copy(src.at[ey], out.at[ey], sems.at[i, ey])
            for i, (src, out) in enumerate(((s_val, val_out), (s_dif, dif_out)))
        ]

    def done(ey):
        for c in copies(ey):
            c.start()

    shifted(
        position()[1] == 1, offs, fetch, (near,), (far, far_end), (near_halo,), vol, lhs, s_val, s_dif, done
    )
    for ey in range(ROW):
        for c in copies(ey):
            c.wait()


def first_kernel(
    near, near_halo, far_halo, val_in, dif_in, warped, w_base, w_step, val, dif, sems
):
    copies = [
        [
            pltpu.make_async_copy(src.at[ey], out.at[ey], sems.at[i, ey])
            for i, (src, out) in enumerate(((val_in, val), (dif_in, dif)))
        ]
        for ey in range(ROW)
    ]
    for pair in copies:
        for c in pair:
            c.start()
    odd = position()[1] == 1
    displacements(odd, near, near_halo, far_halo, w_base, w_step)
    for ey, pair in enumerate(copies):
        for c in pair:
            c.wait()
        interpolate(val, dif, w_base, w_step, jnp.where(odd, 0, HALF), warped, ey)


def second_kernel(
    near, far, far_end, far_halo, far_halo_end, w_base, w_step,
    warp_a, b0, b1, x_bands, y_bands, offs_in,
    warped, residual, y, misfit, vol, lhs, s_val, s_dif, offs, sem, rounded, out_sem,
):
    odd = position()[1] == 1
    fetch = pltpu.make_async_copy(offs_in, offs, sem)
    fetch.start()
    halo = (far_halo, far_halo_end)
    shifted(
        jnp.logical_not(odd), offs, fetch, (far, far_end), (near,), halo, vol, lhs, s_val, s_dif
    )
    for ey in range(ROW):
        interpolate(s_val, s_dif, w_base, w_step, jnp.where(odd, HALF, 0), warped, ey)
    filter_half(
        (0, 1), warp_a, warped, (b0, b1), x_bands, y_bands,
        residual, y, misfit, rounded, out_sem,
    ).wait()


VMEM = pl.BlockSpec(memory_space=pltpu.VMEM)
HBM = pl.BlockSpec(memory_space=pltpu.HBM)
FIELD = jax.ShapeDtypeStruct((3, N, N), jnp.float32)
HALF_VOLUME = jax.ShapeDtypeStruct((HALF, N, N), jnp.float32)
SAMPLES = (ROW, HALF + 1, E + 8, N)
RESIDUAL = jax.ShapeDtypeStruct((E, N, N), jnp.bfloat16)
FILTERED = jax.ShapeDtypeStruct((3, HALF, N, N), jnp.float32)
SMALL = jax.ShapeDtypeStruct((3, 1, (ROW + 1) ** 2), jnp.float32)


def call(kernel, name, outs, vmem, scratch, mib, hbm=(), hbm_outs=(), alias=None):
    specs = [VMEM] * len(vmem)
    return pl.pallas_call(
        kernel,
        out_shape=outs,
        in_specs=specs + [HBM] * len(hbm),
        out_specs=tuple(HBM if i in hbm_outs else VMEM for i in range(len(outs))),
        input_output_aliases=alias or {},
        scratch_shapes=scratch,
        compiler_params=pltpu.CompilerParams(vmem_limit_bytes=mib * 1024 * 1024),
        name=name,
    )(*vmem, *hbm)


def split(nodes, slab):
    return call(
        split_kernel,
        "split",
        tuple(jax.ShapeDtypeStruct((n, N, N), jnp.bfloat16) for n in (HALO + 1, FAR + 1, HALO - FAR)),
        [],
        [
            pltpu.VMEM((1, 3, 1, (ROW + 1) ** 2), jnp.float32),
            pltpu.VMEM((8, N), jnp.float32),
            pltpu.SemaphoreType.DMA((4,)),
        ],
        4,
        hbm=[nodes, slab],
    )


SAMPLE_SCRATCH = [pltpu.VMEM(SAMPLES, jnp.float32)] * 2
WINDOW_SCRATCH = [
    pltpu.VMEM((E + HALO, ROWS, N), jnp.float32),
    pltpu.VMEM((HALF + 1, WIN, 2 * N), jnp.bfloat16),
    *SAMPLE_SCRATCH,
    pltpu.SMEM((3, 1, ROW * ROW), jnp.int32),
    pltpu.SemaphoreType.DMA,
]
EACH_ROW = pltpu.SemaphoreType.DMA((2, ROW))


def windows(offs, planes):
    out = pltpu.HBM(SAMPLES, jnp.float32)
    scratch = WINDOW_SCRATCH + [EACH_ROW]
    return call(
        window_kernel, "windows", (out, out), planes, scratch, 20, hbm=[offs], hbm_outs=(0, 1)
    )


def first_half(planes, samples):
    samples = [pltpu.with_memory_space_constraint(x, pltpu.HBM) for x in samples]
    scratch = SAMPLE_SCRATCH + [EACH_ROW]
    outs = (HALF_VOLUME, FIELD, FIELD)
    return call(first_kernel, "first_half", outs, planes, scratch, 16, hbm=samples)


EDGES = pltpu.VMEM((3, RADIUS + 1, N, N), jnp.float32)
ROUNDED = [pltpu.VMEM((HALF, N, N), jnp.bfloat16), pltpu.SemaphoreType.DMA]


def bands():
    return jnp.asarray(X_BANDS, jnp.bfloat16), jnp.asarray(Y_BANDS, jnp.bfloat16)


def second_half(offs, planes, warp_a, blocks):
    return call(
        second_kernel,
        "second_half",
        (HALF_VOLUME, RESIDUAL, FILTERED, HALF_VOLUME),
        [*planes, warp_a, *blocks, *bands()],
        WINDOW_SCRATCH + ROUNDED,
        32,
        hbm=[offs],
        hbm_outs=(1,),
    )


def filter_into(y, planes, at, x_bands, y_bands):
    count = len(planes)
    smoothed, slopes = [], []
    for i in range(0, count, 2):
        pair = jnp.concatenate(planes[i : i + 2], axis=1)
        along_y = jnp.dot(y_bands[...], pair, preferred_element_type=jnp.float32)
        along_y = along_y.astype(jnp.bfloat16)
        smoothed += [along_y[:N, :N], along_y[:N, N:]]
        slopes.append(along_y[N:])
    rows = pl.ds(at, count)
    out = jnp.dot(jnp.concatenate(smoothed), x_bands[0:N], preferred_element_type=jnp.float32)
    y[0, rows] = out[:, :N].reshape(-1, N, N)
    y[2, rows] = out[:, N:].reshape(-1, N, N)
    out = jnp.dot(jnp.concatenate(slopes), x_bands[N:], preferred_element_type=jnp.float32)
    for i in range(count):
        y[1, at + i] = out[i // 2 * N : i // 2 * N + N, i % 2 * N : i % 2 * N + N]


def filter_half(
    slots, warp_a, warp_b, blocks, x_bands, y_bands, residual, y, misfit, rounded, sem
):
    me, odd = position()
    depth = blocks[0].shape[0]
    half = (me ^ slots[0]) // 2

    def subtract(warped):
        for j, b in zip(slots, blocks):
            at = ((me ^ j) % 2) * depth
            for i in range(depth):
                m = warped[at + i] - b[i].astype(jnp.float32)
                misfit[at + i] = m
                rounded[at + i] = m.astype(jnp.bfloat16)

    pl.when(half + odd == 1)(lambda: subtract(warp_a))
    pl.when(half + odd != 1)(lambda: subtract(warp_b))
    out = pltpu.make_async_copy(rounded, residual.at[pl.ds(half * HALF, HALF)], sem)
    out.start()
    for j, b in zip(slots, blocks):
        at = ((me ^ j) % 2) * depth
        filter_into(y, [b[i] for i in range(depth)], at, x_bands, y_bands)
    return out


def add_up(sums, y, misfit, edges, begin, end):
    smooth = [float(SMOOTH[RADIUS + t] / SMOOTH[RADIUS]) for t in range(RADIUS + 1)]
    slope = [float(SLOPE[RADIUS + t] / SLOPE[RADIUS + 1]) for t in range(RADIUS + 1)]

    def plane(k, z, rows):
        if z < 0:
            return edges[k, RADIUS + z, rows]
        if z >= E:
            return edges[k, z - E, rows]
        return y[z // HALF][k, z % HALF, rows]

    def planes_of(rows):
        window = [[plane(k, begin + t, rows) for t in range(-RADIUS, RADIUS)] for k in range(3)]
        zero = jnp.zeros((8, N), jnp.float32)
        plain = [zero] * 3
        running = [zero] * 3
        for z in range(begin, end):
            for k in range(3):
                window[k] = window[k] + [plane(k, z + RADIUS, rows)]
            m = misfit[z // HALF][z % HALF, rows]
            w = window[0]
            grads = [(w[4] - w[2]) + slope[2] * (w[5] - w[1]) + slope[3] * (w[6] - w[0])]
            for k in (1, 2):
                w = window[k]
                grads.append(
                    w[3]
                    + smooth[1] * (w[4] + w[2])
                    + smooth[2] * (w[5] + w[1])
                    + smooth[3] * (w[6] + w[0])
                )
            for k in range(3):
                plain[k] = plain[k] + grads[k] * m
                running[k] = running[k] + plain[k]
                window[k] = window[k][1:]
        return plain, [plain[k] * ((end + 0.5) / E) - running[k] * (1.0 / E) for k in range(3)]

    def rows_of(r, carry):
        rows = pl.ds(pl.multiple_of(r * 8, 8), 8)
        ey = r // (E // 8)
        plains, uppers = planes_of(rows)
        row = lax.broadcasted_iota(jnp.int32, (8, N), 0) + (r % (E // 8)) * 8
        py = (row.astype(jnp.float32) + 0.5) * (1.0 / E)
        for k in range(3):
            for iz, part in enumerate((plains[k] - uppers[k], uppers[k])):
                right = part * py
                sums[ey, iz * 3 + k] += part - right
                sums[ey + 1, iz * 3 + k] += right
        return carry

    lax.fori_loop(0, N // 8, rows_of, 0, unroll=4 if end - begin == RADIUS else 1)


def in_each_case(add, low, high, near_end):
    me, odd = position()
    for first_low in (True, False):
        for start in (True, False):
            parts = (low, high) if first_low else (high, low)
            case = ((me < 2) == first_low) & ((odd == 1) == (start == near_end))
            inner = (0, E - RADIUS) if start else (RADIUS, E)
            outer = (0, RADIUS) if start else (E - RADIUS, E)
            pl.when(case)(
                lambda parts=parts, planes=inner if near_end else outer: add(*zip(*parts), *planes)
            )


def inner_kernel(
    warp_a, warp_b, b2, b3, edge, y_a, misfit_a, x_bands, y_bands, residual_in,
    residual, y, misfit, sums, rounded, sem, edges,
):
    out = filter_half(
        (2, 3), warp_a, warp_b, (b2, b3), x_bands, y_bands,
        residual, y, misfit, rounded, sem,
    )
    sums[...] = jnp.zeros_like(sums)
    planes = [edge[i] for i in (0, 1, 2, 2)]
    filter_into(edges, planes, 0, x_bands, y_bands)
    in_each_case(
        lambda ys, misfits, begin, end: add_up(sums, ys, misfits, edges, begin, end),
        (y_a, misfit_a), (y, misfit), True,
    )
    out.wait()


def outer_kernel(
    edge, y_a, misfit_a, y_b, misfit_b, earlier, x_bands, y_bands, hats,
    bottom, top, edges, sums,
):
    planes = [edge[i] for i in (0, 1, 2, 2)]
    filter_into(edges, planes, 0, x_bands, y_bands)
    sums[...] = earlier[...]
    in_each_case(
        lambda ys, misfits, begin, end: add_up(sums, ys, misfits, edges, begin, end),
        (y_a, misfit_a), (y_b, misfit_b), False,
    )
    pieces = []
    for iy in range(ROW + 1):
        rest = sums[iy].reshape(48, N)
        three = []
        for _ in range(3):
            three.append(rest.astype(jnp.bfloat16))
            rest = rest - three[-1].astype(jnp.float32)
        pieces.append(jnp.concatenate(three))
    out = jnp.dot(
        jnp.concatenate(pieces, axis=1), hats[...], preferred_element_type=jnp.float32
    )
    out = out[:48] + out[48:96] + out[96:]
    out = jnp.sum(out.reshape(6, 8, N), axis=1)
    for k in range(3):
        gain = float(SLOPE[RADIUS + 1] if k == 0 else SMOOTH[RADIUS]) / E
        bottom[k] = out[k : k + 1, : (ROW + 1) ** 2] * gain
        top[k] = out[3 + k : 4 + k, : (ROW + 1) ** 2] * gain


SUMS = jax.ShapeDtypeStruct((ROW + 1, 6, 8, N), jnp.float32)


def inner(halves, blocks, edge, lower, residual):
    return call(
        inner_kernel,
        "inner",
        (RESIDUAL, FILTERED, HALF_VOLUME, SUMS),
        [*halves, *blocks, edge, *lower, *bands()],
        ROUNDED + [EDGES],
        32,
        hbm=[residual],
        hbm_outs=(0,),
        alias={9: 0},
    )


def assemble(edge, halves, earlier):
    return call(
        outer_kernel,
        "outer",
        (SMALL, SMALL),
        [
            edge, *halves, earlier,
            *bands(),
            jnp.asarray(RHS_HATS.reshape(-1, N), jnp.bfloat16),
        ],
        [
            EDGES,
            pltpu.VMEM(SUMS.shape, jnp.float32),
        ],
        24,
    )


def body(tomogram, deformed, subvoxel, offsets):
    bricks = lax.axis_size("brick")
    me = lax.axis_index("scan")
    odd = lax.axis_index("brick") % 2
    up = [(i, i + 1) for i in range(bricks - 1)]
    inside = [r for i in range(0, bricks - 1, 2) for r in ((i, i + 1), (i + 1, i))]
    outside = [r for i in range(1, bricks - 1, 2) for r in ((i, i + 1), (i + 1, i))]
    pairs = [(0, 1), (1, 0), (2, 3), (3, 2)]

    slab = pltpu.with_memory_space_constraint(deformed, pltpu.HBM)
    across = lax.ppermute(tomogram, "scan", [(0, 2), (1, 3), (2, 0), (3, 1)])
    near, far, far_end = split(pltpu.with_memory_space_constraint(subvoxel, pltpu.HBM), slab)
    offs = pltpu.with_memory_space_constraint(offsets.reshape(3, 1, -1), pltpu.HBM)
    halo_a = lax.ppermute(near, "brick", inside)
    halo_b = lax.ppermute(far, "brick", outside)
    halo_c = lax.ppermute(far_end, "brick", outside)
    late = tomogram
    beside = lax.ppermute(late, "scan", pairs)
    slab_parts = (near, far, far_end)
    samples = windows(offs, (*slab_parts, halo_a))
    across, samples = lax.optimization_barrier((across, samples))
    relayed = lax.ppermute(across, "scan", pairs)
    blocks = (tomogram, beside, across, relayed)
    warp_a, *field = first_half((near, halo_a, halo_b), samples)
    warp_b, residual, *lower = second_half(
        offs, (*slab_parts, halo_b, halo_c, *field), warp_a, blocks[:2]
    )
    halves = (warp_a, warp_b)

    def pick(index, part):
        out = part(blocks[0])
        for j in range(1, 4):
            out = jnp.where((me ^ j) == index, part(blocks[j]), out)
        return out

    tail, head = pick(3, lambda b: b[-RADIUS:]), pick(0, lambda b: b[:RADIUS])
    send_a, send_b, lower[0] = lax.optimization_barrier(
        (jnp.where(odd == 1, head, tail), jnp.where(odd == 1, tail, head), lower[0])
    )
    edge_a = lax.ppermute(send_a, "brick", inside)
    edge_b = lax.ppermute(send_b, "brick", outside)
    residual, y, misfit, sums = inner(halves, blocks[2:], edge_a, lower, residual)
    bottom, top = assemble(edge_b, (*lower, y, misfit), sums)
    node_rhs = bottom + lax.ppermute(top, "brick", up)
    return residual[None], node_rhs[None]


def solution(mesh):
    return jax.shard_map(
        body,
        mesh=mesh,
        in_specs=(
            P(("brick", "scan"), None, None),
            P("scan", "brick", None, None),
            P("scan", None, "brick", None),
            P("scan", None, "brick"),
        ),
        out_specs=(P("scan", "brick", None, None), P("scan", None, "brick", None)),
        check_vma=False,
    )
```
